256 devices in a mesh: shot: 16 (over y_lo, z), slab: 16 (over y_hi, x, core).
Axes of the slice: x: 4, y: 4 (y_hi: 2, y_lo: 2; y = y_hi * 2 + y_lo), z: 8, core: 2. Of those that a mesh axis runs over, the one named last changes fastest.
Arguments:
- courant: float32 [256, 128, 128], P('slab'), may hold values from 0.225 to 0.45
- adj_prev: float32 [32, 256, 128, 128], P('shot', 'slab'), may hold values from -10 to 10
- adj_curr: float32 [32, 256, 128, 128], P('shot', 'slab'), may hold values from -8 to 8
- forward_snaps: bfloat16 [32, 2, 256, 128, 128], P('shot', None, 'slab'), may hold values from -6 to 6
- traces: float32 [32, 2, 128], P('shot'), may hold values from -12 to 12
- receiver_z: int32 [32, 128], P('shot'), may hold values from 0 to 255
- receiver_x: int32 [32, 128], P('shot'), may hold values from 0 to 127
- receiver_y: int32 [32, 128], P('shot'), may hold values from 0 to 127
- pml_cells: int32 [3], replicated, may hold values from 4 to 11
- omega_z: int32 [256, 128], P('slab'), may hold values from -2 to 2
- omega_x: int32 [128, 128], replicated, may hold values from -2 to 2
- omega_y: int32 [128, 128], replicated, may hold values from -2 to 2
Outputs:
- sketch: float32 [32, 128], P('shot')
- coarse: float32 [32, 256, 8192], P('shot', 'slab')
- gram_band: float32 [32, 4, 2], P('shot')
The draws below stay inside these ranges and needn't reach their ends.
All inputs are finite; a program needn't handle non-finite values.
Results may differ from the reference program's by a relative error of at most 0.0047.
Values sent between devices are 32-bit elements; how exact they have to be, the bound alone decides.
No kernel may reach another device: no remote copies, remote signals or barrier semaphores. Data moves between devices by JAX's collectives and lax.ppermute only.
A program may use at most 128 MiB of HBM per device.

```python
import math
import jax
import jax.numpy as jnp
from jax import lax

CZ = 16
NX = 128
NY = 128
SHOT_DEV = 2
RECV = 128
STEPS = 2
RANK = 128
LAGS = 4
NZ = 256
SHOTS = 32
N_SHOT = 16


def wave_field(key, scale_low, scale_high):
    limit = 2.0 * math.pi / 32.0
    wave_z = jax.random.uniform(jax.random.fold_in(key, 101), (SHOTS, 4), jnp.float32, -limit, limit)
    wave_x = jax.random.uniform(jax.random.fold_in(key, 102), (SHOTS, 4), jnp.float32, -limit, limit)
    wave_y = jax.random.uniform(jax.random.fold_in(key, 103), (SHOTS, 4), jnp.float32, -limit, limit)
    phases = jax.random.uniform(jax.random.fold_in(key, 104), (SHOTS, 4), jnp.float32, 0.0, 2.0 * math.pi)
    depth_cells = jnp.arange(NZ, dtype=jnp.float32)
    cells_x = jnp.arange(NX, dtype=jnp.float32)
    cells_y = jnp.arange(NY, dtype=jnp.float32)
    wave_total = jnp.zeros((SHOTS, NZ, NX, NY), jnp.float32)
    for member in range(4):
        angle_sum = wave_z[:, member][:, None, None, None] * depth_cells[None, :, None, None] + wave_x[:, member][:, None, None, None] * cells_x[None, None, :, None] + wave_y[:, member][:, None, None, None] * cells_y[None, None, None, :] + phases[:, member][:, None, None, None]
        wave_total = wave_total + jnp.cos(angle_sum)
    smooth_part = math.sqrt(0.5) * wave_total
    position = (jnp.arange(NZ, dtype=jnp.int32) % CZ).astype(jnp.float32)
    distance = jnp.minimum(position + 0.5, CZ - position - 0.5)
    envelope = 0.1 + 0.9 * jnp.exp(-jnp.square(jnp.maximum(distance - 2.5, 0.0) / 1.2))
    rough_part = jnp.clip(jax.random.normal(jax.random.fold_in(key, 105), (SHOTS, NZ, NX, NY), jnp.float32), -6.0, 6.0)
    shot_scale = jnp.exp(jax.random.uniform(jax.random.fold_in(key, 106), (SHOTS,), jnp.float32, math.log(scale_low), math.log(scale_high)))
    return shot_scale[:, None, None, None] * envelope[None, :, None, None] * (smooth_part + 0.05 * rough_part)


def draw_adj_curr(key, part):
    field_now = wave_field(key, 1.0, 1.0)
    return jnp.clip(field_now, -8.0, 8.0)


def draw_adj_prev(key, part):
    field_now = wave_field(key, 1.0, 1.0)
    key = jax.random.fold_in(key, 5)
    factor = jax.random.uniform(jax.random.fold_in(key, 1), (SHOTS, NZ, NX, NY), jnp.float32, 1.5, 1.7)
    extra = jnp.clip(jax.random.normal(jax.random.fold_in(key, 2), (SHOTS, NZ, NX, NY), jnp.float32), -6.0, 6.0)
    return jnp.clip(factor * jnp.clip(field_now, -8.0, 8.0) + 0.02 * extra, -10.0, 10.0)


def draw_courant(key, part):
    key = jax.random.fold_in(key, 7)
    uniform_cells = jax.random.uniform(key, (NZ, NX, NY), jnp.float32)
    power = 6.0
    return 0.45 * (1.0 - 0.5 * uniform_cells ** power)


def set_ends(array, key, least, high):
    dims = array.shape
    index_at = [jax.random.randint(jax.random.fold_in(key, axis), (), 0, dims[axis]) for axis in range(len(dims))]
    array = array.at[tuple(index_at)].set(least)
    longest = dims.index(max(dims))
    index_at[longest] = (index_at[longest] + 1) % dims[longest]
    return array.at[tuple(index_at)].set(high)


def block_levels(rng, shape, pieces, smallest, top_value):
    loudness, own = 1.0, jax.random.fold_in(rng, 6)
    for dim, parts in pieces:
        draws = jnp.exp(jax.random.uniform(jax.random.fold_in(own, dim), (parts,), jnp.float32, smallest / len(pieces), top_value / len(pieces)))
        loudness = loudness * jnp.repeat(draws, shape[dim] // parts).reshape([-1 if axis == dim else 1 for axis in range(len(shape))])
    return loudness


def normal_values(own_key, dims, deviation, most, split=(), held_as=jnp.bfloat16):
    values = jax.random.normal(own_key, dims, jnp.float32) * deviation
    if len(split) > 0:
        values = block_levels(own_key, dims, split, -0.22, 0.18) * values
    return jnp.clip(values, min=-most, max=most).astype(held_as)


def setup_inputs(seed: int = 0) -> dict:
    splits = jax.random.split(jax.random.key(seed), 13)
    courant = draw_courant(jax.random.fold_in(splits[12], 71), 0)
    adj_prev = draw_adj_prev(jax.random.fold_in(splits[12], 71), 0)
    adj_curr = draw_adj_curr(jax.random.fold_in(splits[12], 71), 0)
    forward_snaps = normal_values(splits[3], (SHOTS, STEPS, NZ, NX, NY), 1.0, 6.0, ((0, 16), (2, 16)))
    traces = normal_values(splits[4], (SHOTS, STEPS, RECV), 2.0, 12.0, ((0, 16),), jnp.float32)
    receiver_z = set_ends(jax.random.randint(splits[5], (SHOTS, RECV), 0, NZ), jax.random.fold_in(splits[5], 1), 0, NZ - 1).astype(jnp.int32)
    receiver_x = set_ends(jax.random.randint(splits[6], (SHOTS, RECV), 0, NX), jax.random.fold_in(splits[6], 1), 0, NX - 1).astype(jnp.int32)
    receiver_y = set_ends(jax.random.randint(splits[7], (SHOTS, RECV), 0, NY), jax.random.fold_in(splits[7], 1), 0, NY - 1).astype(jnp.int32)
    pml_cells = jax.random.randint(splits[8], (3,), 4, 12).astype(jnp.int32)
    omega_z = set_ends(jax.random.randint(splits[9], (NZ, RANK), -2, 3), jax.random.fold_in(splits[9], 1), -2, 2).astype(jnp.int32)
    omega_x = set_ends(jax.random.randint(splits[10], (NX, RANK), -2, 3), jax.random.fold_in(splits[10], 1), -2, 2).astype(jnp.int32)
    omega_y = set_ends(jax.random.randint(splits[11], (NY, RANK), -2, 3), jax.random.fold_in(splits[11], 1), -2, 2).astype(jnp.int32)
    return dict(courant=courant, adj_prev=adj_prev, adj_curr=adj_curr, forward_snaps=forward_snaps, traces=traces, receiver_z=receiver_z, receiver_x=receiver_x, receiver_y=receiver_y, pml_cells=pml_cells, omega_z=omega_z, omega_x=omega_x, omega_y=omega_y)


stencil_coeffs = (-205.0 / 72.0, 8.0 / 5.0, -1.0 / 5.0, 8.0 / 315.0, -1.0 / 560.0)
damp_peak = 0.3

def pml_ramp(position, length, thickness):
    distance = jnp.minimum(position, length - 1 - position).astype(jnp.float32)
    reach = thickness.astype(jnp.float32)
    return jnp.maximum((reach - distance) / reach, 0.0)

def damping_field(index_z, index_x, index_y, total_z, cells_x, cells_y, pml_cells):
    ramp_z = pml_ramp(index_z, total_z, pml_cells[0])
    ramp_x = pml_ramp(index_x, cells_x, pml_cells[1])
    ramp_y = pml_ramp(index_y, cells_y, pml_cells[2])
    return damp_peak * (ramp_z[:, None, None] * ramp_z[:, None, None] + ramp_x[None, :, None] * ramp_x[None, :, None] + ramp_y[None, None, :] * ramp_y[None, None, :])

def laplace(extended, values):
    cells_z, cells_x, cells_y = values.shape[-3:]
    leading = [(0, 0)] * (values.ndim - 3)
    padded = jnp.pad(extended, leading + [(0, 0), (4, 4), (4, 4)])
    total = 3.0 * stencil_coeffs[0] * values
    for offset in range(1, 5):
        weight = stencil_coeffs[offset]
        along_z = padded[..., 4 + offset:4 + offset + cells_z, 4:4 + cells_x, 4:4 + cells_y] + padded[..., 4 - offset:4 - offset + cells_z, 4:4 + cells_x, 4:4 + cells_y]
        along_x = padded[..., 4:4 + cells_z, 4 + offset:4 + offset + cells_x, 4:4 + cells_y] + padded[..., 4:4 + cells_z, 4 - offset:4 - offset + cells_x, 4:4 + cells_y]
        along_y = padded[..., 4:4 + cells_z, 4:4 + cells_x, 4 + offset:4 + offset + cells_y] + padded[..., 4:4 + cells_z, 4:4 + cells_x, 4 - offset:4 - offset + cells_y]
        total = total + weight * (along_z + along_x + along_y)
    return total

def reference(courant, adj_prev, adj_curr, forward_snaps, traces, receiver_z, receiver_x, receiver_y, pml_cells, omega_z, omega_x, omega_y):
    highest = lax.Precision.HIGHEST
    total_z, cells_x, cells_y = courant.shape
    index_z = jnp.arange(total_z, dtype=jnp.int32)
    index_x = jnp.arange(cells_x, dtype=jnp.int32)
    index_y = jnp.arange(cells_y, dtype=jnp.int32)
    damping = damping_field(index_z, index_x, index_y, total_z, cells_x, cells_y, pml_cells)
    speed_sq = courant * courant
    sketch_scale = 1.0 / math.sqrt(total_z * cells_x * cells_y)
    gram_scale = 1.0 / math.sqrt(total_z * cells_x * cells_y // 2)
    omega_zf = omega_z.astype(jnp.float32)
    omega_xf = omega_x.astype(jnp.float32)
    omega_yf = omega_y.astype(jnp.float32)

    def one_shot(shot_items):
        previous, current, snaps, trace_rows, place_z, place_x, place_y = shot_items
        gradient = jnp.zeros((total_z, cells_x, cells_y), jnp.float32)
        for instant in range(STEPS):
            source = jnp.zeros((total_z, cells_x, cells_y), jnp.float32).at[place_z, place_x, place_y].add(trace_rows[instant])
            extended = jnp.pad(current, ((4, 4), (0, 0), (0, 0)))
            updated = (2.0 * current - (1.0 - damping) * previous + speed_sq * laplace(extended, current) + source) / (1.0 + damping)
            gradient = gradient + updated * snaps[instant].astype(jnp.float32)
            previous, current = (current, updated)
        rounded = lax.optimization_barrier(gradient.astype(jnp.bfloat16))
        widened = rounded.astype(jnp.float32)
        first = jnp.einsum('zxy,yr->zxr', widened, omega_yf, precision=highest)
        second = jnp.einsum('zxr,xr->zr', first, omega_xf, precision=highest)
        partial_sketch = lax.optimization_barrier(jnp.sum(second * omega_zf, axis=0))
        coarse_shot = (0.5 * (widened[:, :, 0::2] + widened[:, :, 1::2])).reshape(total_z, cells_x * cells_y // 2)
        return (partial_sketch, coarse_shot)
    sketch, coarse = lax.map(one_shot, (adj_prev, adj_curr, forward_snaps, traces, receiver_z, receiver_x, receiver_y))
    sketch = sketch * sketch_scale
    panels = coarse.reshape(N_SHOT, SHOT_DEV, total_z * cells_x * cells_y // 2)
    bands = []
    for lag_index in range(LAGS):
        partner = jnp.roll(panels, lag_index + 1, axis=0)
        bands.append(jnp.einsum('gic,gjc->gij', panels, partner, precision=highest))
    gram_band = jnp.stack(bands, axis=2).reshape(N_SHOT * SHOT_DEV, LAGS, SHOT_DEV) * gram_scale
    return (sketch, coarse, gram_band)
```

```python
import functools
import math

import jax
import jax.numpy as jnp
import ml_dtypes
import numpy as np
from jax import lax
from jax.experimental import pallas as pl
from jax.experimental.pallas import tpu as pltpu
from jax.sharding import PartitionSpec as P

LAGS = 4
REACH = 4
TAPS = (-205.0 / 72.0, 8.0 / 5.0, -1.0 / 5.0, 8.0 / 315.0, -1.0 / 560.0)
CENTRE = 3.0 * TAPS[0]
DAMP_PEAK = 0.3
F32 = jnp.float32
BF16 = jnp.bfloat16
VMEM_BYTES = 24 * 1024 * 1024


def band_parts(cells):
    index = np.arange(cells)
    apart = np.abs(index[:, None] - index[None, :])
    band = np.zeros((cells, cells), np.float32)
    for offset in range(1, REACH + 1):
        band[apart == offset] = TAPS[offset]
    high = band.astype(ml_dtypes.bfloat16)
    low = (band - high.astype(np.float32)).astype(ml_dtypes.bfloat16)
    return high, low


def pool_matrix(cells_y):
    half = cells_y // 2
    pool = np.zeros((2 * cells_y, 2 * half), np.float32)
    index = np.arange(cells_y)
    pool[index, index // 2] = 0.5
    pool[cells_y + index, half + index // 2] = 0.5
    return pool.astype(ml_dtypes.bfloat16)


def dot(left, right):
    return lax.dot_general(left, right, (((1,), (0,)), ((), ())), preferred_element_type=F32)


def dot_rows(left, right):
    return lax.dot_general(left, right, (((1,), (1,)), ((), ())), preferred_element_type=F32)


def two_parts(values):
    high = values.astype(BF16)
    low = (values - high.astype(F32)).astype(BF16)
    return high, low


def along_xy(plane, band_y, band_x):
    high, low = two_parts(plane)
    return dot(jnp.concatenate([high, low, high], axis=1), band_y) + dot(
        band_x, jnp.concatenate([high, low, high], axis=0)
    )


def ramp_squared(index, length, thickness):
    distance = jnp.minimum(index, length - 1 - index).astype(F32)
    reach = jnp.full(index.shape, thickness, jnp.int32).astype(F32)
    ramp = jnp.maximum((reach - distance) / reach, 0.0)
    return ramp * ramp


def begin_kernel(
    total_z,
    pml,
    courant,
    prev,
    curr,
    traces,
    place_z,
    place_x,
    place_y,
    band_y,
    band_x,
    updated,
    rest,
    gain_self,
    gain_lap,
    ramp_z,
    ramp_xy,
    inject,
):
    cells_z, cells_x, cells_y = courant.shape
    shots = curr.shape[0]
    first_z = lax.axis_index("slab") * cells_z
    plane = (cells_x, cells_y)
    row = lax.broadcasted_iota(jnp.int32, plane, 0)
    column = lax.broadcasted_iota(jnp.int32, plane, 1)
    ramp_z[...] = ramp_squared(
        lax.broadcasted_iota(jnp.int32, ramp_z.shape, 0) + first_z, total_z, pml[0]
    )
    ramp_xy[...] = ramp_squared(row, cells_x, pml[1]) + ramp_squared(column, cells_y, pml[2])
    receivers = traces.shape[2]
    for shot in range(shots):
        cell = lax.broadcasted_iota(jnp.int32, (cells_y, receivers), 0)
        here = cell == place_y[shot : shot + 1, :]
        for instant in range(2):
            high, low = two_parts(jnp.where(here, traces[shot, instant : instant + 1, :], 0.0))
            span = slice(instant * cells_y, (instant + 1) * cells_y)
            inject[shot, span, :receivers] = high
            inject[shot, span, receivers:] = low
    line = lax.broadcasted_iota(jnp.int32, (cells_x, receivers), 0)

    @pl.loop(0, cells_z)
    def _(z):
        damping = DAMP_PEAK * (ramp_z[pl.ds(z, 1), :] + ramp_xy[...])
        scale = 1.0 / (1.0 + damping)
        speed = courant[z]
        lap_gain = scale * (speed * speed)
        self_gain = 2.0 * scale + CENTRE * lap_gain
        prev_gain = scale * (1.0 - damping)
        gain_self[z] = self_gain
        gain_lap[z] = lap_gain
        for shot in range(shots):
            now = curr[shot, z]
            lap = along_xy(now, band_y[...], band_x[...])
            for offset in range(1, REACH + 1):
                below = jnp.where(z - offset >= 0, TAPS[offset], 0.0)
                above = jnp.where(z + offset < cells_z, TAPS[offset], 0.0)
                lap += below * curr[shot, jnp.maximum(z - offset, 0)]
                lap += above * curr[shot, jnp.minimum(z + offset, cells_z - 1)]
            code = (place_z[shot : shot + 1, :] - first_z - z) * cells_x + place_x[shot : shot + 1, :]
            mark = jnp.where(line == code, 1.0, 0.0).astype(BF16)
            source = dot_rows(jnp.concatenate([mark, mark], axis=1), inject[shot])
            updated[shot, z] = (
                self_gain * now
                - prev_gain * prev[shot, z]
                + lap_gain * lap
                + scale * source[:, :cells_y]
            )
            rest[shot, z] = scale * source[:, cells_y:] - prev_gain * now


def halo_terms(halo, shot, layer, upper):
    total = None
    for offset in range(1, REACH + 1):
        at = layer + offset - REACH if upper else layer - offset + REACH
        if 0 <= at < REACH:
            term = TAPS[offset] * halo[shot, at]
            total = term if total is None else total + term
    return total


def edge_kernel(upper, partial, halo, gain_lap, out):
    @pl.loop(0, partial.shape[0])
    def _(shot):
        for layer in range(REACH):
            out[shot, layer] = partial[shot, layer] + gain_lap[layer] * halo_terms(
                halo, shot, layer, upper
            )


def emit(gradient, shot, layer, spread_y, weight_z, pool, chunks, total, lines):
    rounded = gradient.astype(BF16)
    total[shot] += dot(rounded, spread_y[...]) * weight_z
    lines[...] = rounded.astype(F32)
    half = lines.shape[0] // 2
    even = lines[pl.ds(0, half, stride=2), :].astype(BF16)
    odd = lines[pl.ds(1, half, stride=2), :].astype(BF16)
    coarse = dot(jnp.concatenate([even, odd], axis=1), pool[...])
    part = chunks.shape[2]
    pieces = half // part
    for piece in range(pieces):
        chunks[layer * pieces + piece, shot] = coarse[piece * part : (piece + 1) * part]


def middle_kernel(
    partial,
    low,
    high,
    rest,
    gain_self,
    gain_lap,
    snaps,
    omega_z,
    omega_x,
    omega_y,
    band_y,
    band_x,
    pool,
    chunks,
    edge_low,
    edge_high,
    sketch,
    wave,
    total,
    spread_y,
    lines,
    sems,
):
    shots, cells_z = wave.shape[:2]
    last = cells_z - REACH
    copies = [
        pltpu.make_async_copy(low, wave.at[:, pl.ds(0, REACH)], sems.at[0]),
        pltpu.make_async_copy(
            partial.at[:, pl.ds(REACH, last - REACH)],
            wave.at[:, pl.ds(REACH, last - REACH)],
            sems.at[1],
        ),
        pltpu.make_async_copy(high, wave.at[:, pl.ds(last, REACH)], sems.at[2]),
    ]
    for copy in copies:
        copy.start()
    spread_y[...] = omega_y[...].astype(F32).astype(BF16)
    total[...] = jnp.zeros_like(total)
    for copy in copies:
        copy.wait()

    def gradient_at(shot, z, lap):
        now = wave[shot, z]
        later = gain_self[z] * now + rest[shot, z] + gain_lap[z] * lap
        return now * snaps[shot, 0, z].astype(F32) + later * snaps[shot, 1, z].astype(F32)

    @pl.loop(REACH, last)
    def _(z):
        weight_z = omega_z[pl.ds(z, 1), :].astype(F32)
        for shot in range(shots):
            lap = along_xy(wave[shot, z], band_y[...], band_x[...])
            for offset in range(1, REACH + 1):
                lap += TAPS[offset] * (wave[shot, z - offset] + wave[shot, z + offset])
            emit(
                gradient_at(shot, z, lap),
                shot,
                z - REACH,
                spread_y,
                weight_z,
                pool,
                chunks,
                total,
                lines,
            )

    @pl.loop(0, shots)
    def _(shot):
        for layer in range(REACH):
            for upper in (False, True):
                z = last + layer if upper else layer
                lap = along_xy(wave[shot, z], band_y[...], band_x[...])
                for offset in range(1, REACH + 1):
                    around = [
                        wave[shot, at]
                        for at in (z - offset, z + offset)
                        if 0 <= at < cells_z
                    ]
                    lap += TAPS[offset] * sum(around[1:], around[0])
                (edge_high if upper else edge_low)[shot, layer] = gradient_at(shot, z, lap)

    weights_x = omega_x[...].astype(F32)
    for shot in range(shots):
        sketch[shot : shot + 1, :] = jnp.sum(total[shot] * weights_x, axis=0, keepdims=True)


def finish_kernel(
    edge_low,
    edge_high,
    halo_low,
    halo_high,
    gain_low,
    gain_high,
    snaps_low,
    snaps_high,
    omega_z,
    omega_x,
    omega_y,
    pool,
    before,
    chunks,
    sketch,
    total,
    spread_y,
    lines,
):
    shots = edge_low.shape[0]
    cells_z = omega_z.shape[0]
    spread_y[...] = omega_y[...].astype(F32).astype(BF16)
    total[...] = jnp.zeros_like(total)
    sides = (
        (edge_low, halo_low, gain_low, snaps_low, False),
        (edge_high, halo_high, gain_high, snaps_high, True),
    )

    @pl.loop(0, shots)
    def _(shot):
        for layer in range(REACH):
            for edge, halo, gain, snaps, upper in sides:
                z = cells_z - REACH + layer if upper else layer
                terms = gain[layer] * halo_terms(halo, shot, layer, upper)
                gradient = edge[shot, layer] + terms * snaps[shot, 0, layer].astype(F32)
                emit(
                    gradient,
                    shot,
                    layer + (REACH if upper else 0),
                    spread_y,
                    omega_z[z : z + 1, :].astype(F32),
                    pool,
                    chunks,
                    total,
                    lines,
                )

    weights_x = omega_x[...].astype(F32)
    for shot in range(shots):
        sketch[shot : shot + 1, :] = before[shot : shot + 1, :] + jnp.sum(
            total[shot] * weights_x, axis=0, keepdims=True
        )


def gram_kernel(first, second, out):
    shots = out.shape[0]
    part = first.shape[0] // shots
    gram = jnp.zeros((2 * shots, 2 * shots), F32)
    for chunk in (first, second):

        def add(step, gram):
            rows = [
                chunk[pl.ds(2 * step + index, shots, stride=part), :] for index in range(2)
            ]
            high, low = two_parts(jnp.concatenate(rows, axis=1))
            both = jnp.concatenate([high, low], axis=0)
            return gram + dot_rows(both, both)

        gram = lax.fori_loop(0, part // 2, add, gram)
    folded = (gram[:shots, :shots] + gram[shots:, shots:]) + (
        gram[:shots, shots:] + gram[shots:, :shots]
    )
    out[...] = jnp.zeros_like(out)
    out[:, :shots] = folded


def spec(block=None, index=None):
    if block is None:
        return pl.BlockSpec(memory_space=pltpu.VMEM)
    return pl.BlockSpec(block, lambda step: index)


def run(kernel, out_shape, in_specs=None, out_specs=None, scratch=(), flops=0, moved=0, grid=None):
    options = {}
    if grid is not None:
        options["grid"] = grid
    return pl.pallas_call(
        kernel,
        out_shape=out_shape,
        in_specs=in_specs,
        out_specs=out_specs,
        scratch_shapes=scratch,
        compiler_params=pltpu.CompilerParams(vmem_limit_bytes=VMEM_BYTES),
        cost_estimate=pl.CostEstimate(flops=flops, bytes_accessed=moved, transcendentals=0),
        **options,
    )


def local(
    courant,
    adj_prev,
    adj_curr,
    forward_snaps,
    traces,
    receiver_z,
    receiver_x,
    receiver_y,
    pml_cells,
    omega_z,
    omega_x,
    omega_y,
):
    shots, cells_z, cells_x, cells_y = adj_curr.shape
    slabs = lax.axis_size("slab")
    groups = lax.axis_size("shot")
    total_z = cells_z * slabs
    last = cells_z - REACH
    inner = last - REACH
    rank = omega_z.shape[1]
    receivers = traces.shape[2]
    half_x = cells_x // 2
    part = inner * half_x // groups
    shape = jax.ShapeDtypeStruct
    plane = (cells_x, cells_y)
    high, low = band_parts(cells_y)
    band_y = jnp.asarray(np.concatenate([high, high, low], axis=0))
    high, low = band_parts(cells_x)
    band_x = jnp.asarray(np.concatenate([high, high, low], axis=1))
    pool = jnp.asarray(pool_matrix(cells_y))

    def from_below(layers):
        return lax.ppermute(layers, "slab", [(i, i + 1) for i in range(slabs - 1)])

    def from_above(layers):
        return lax.ppermute(layers, "slab", [(i + 1, i) for i in range(slabs - 1)])

    halo_low = from_below(adj_curr[:, last:])
    halo_high = from_above(adj_curr[:, :REACH])

    vmem = spec()
    field = shape((shots, cells_z) + plane, F32)
    gain = shape((cells_z,) + plane, F32)
    edge = shape((shots, REACH) + plane, F32)
    updated, rest, gain_self, gain_lap = run(
        functools.partial(begin_kernel, total_z),
        [field, field, gain, gain],
        in_specs=[pl.BlockSpec(memory_space=pltpu.SMEM)] + [vmem] * 9,
        out_specs=[vmem] * 4,
        scratch=[
            pltpu.VMEM((cells_z, cells_y), F32),
            pltpu.VMEM(plane, F32),
            pltpu.VMEM((shots, 2 * cells_y, 2 * receivers), BF16),
        ],
        flops=2 * 10**9,
        moved=11 * 2**20,
    )(
        pml_cells,
        courant,
        adj_prev,
        adj_curr,
        traces,
        receiver_z,
        receiver_x,
        receiver_y,
        band_y,
        band_x,
    )

    layers4 = (shots, REACH) + plane
    gains4 = (REACH,) + plane

    def complete(halo, upper):
        side = last // REACH if upper else 0
        return run(
            functools.partial(edge_kernel, upper),
            edge,
            in_specs=[
                spec(layers4, (0, side, 0, 0)),
                spec(layers4, (0, 0, 0, 0)),
                spec(gains4, (side, 0, 0)),
            ],
            out_specs=spec(layers4, (0, 0, 0, 0)),
            grid=(1,),
            flops=10**7,
            moved=2 * 2**20,
        )(updated, halo, gain_lap)

    edge_low = complete(halo_low, False)
    edge_high = complete(halo_high, True)
    next_high = from_above(edge_low)
    next_low = from_below(edge_high)

    chunk = shape((groups, shots, part, cells_y), F32)
    any_space = pl.BlockSpec(memory_space=pl.ANY)
    scratch_emit = [
        pltpu.VMEM((shots, cells_x, rank), F32),
        pltpu.VMEM((cells_y, rank), BF16),
        pltpu.VMEM(plane, F32),
    ]
    chunks_mid, part_low, part_high, sketch_mid = run(
        middle_kernel,
        [chunk, edge, edge, shape((shots, rank), F32)],
        in_specs=[any_space] * 3 + [vmem] * 10,
        out_specs=[vmem] * 4,
        scratch=[pltpu.VMEM((shots, cells_z) + plane, F32)]
        + scratch_emit
        + [pltpu.SemaphoreType.DMA((3,))],
        flops=2 * 10**9,
        moved=11 * 2**20,
    )(
        updated,
        edge_low,
        edge_high,
        rest,
        gain_self,
        gain_lap,
        forward_snaps,
        omega_z,
        omega_x,
        omega_y,
        band_y,
        band_x,
        pool,
    )
    got_mid = lax.all_to_all(chunks_mid, "shot", 0, 0, tiled=True)

    snap4 = (shots, 1, REACH) + plane
    top = last // REACH
    whole2 = lambda array: spec(array.shape, (0,) * array.ndim)
    chunks_edge, sketch_part = run(
        finish_kernel,
        [chunk, shape((shots, rank), F32)],
        in_specs=[spec(layers4, (0, 0, 0, 0))] * 4
        + [
            spec(gains4, (0, 0, 0)),
            spec(gains4, (top, 0, 0)),
            spec(snap4, (0, 1, 0, 0, 0)),
            spec(snap4, (0, 1, top, 0, 0)),
        ]
        + [whole2(omega_z), whole2(omega_x), whole2(omega_y), whole2(pool), whole2(sketch_mid)],
        out_specs=[spec(chunk.shape, (0, 0, 0, 0)), spec((shots, rank), (0, 0))],
        scratch=scratch_emit,
        grid=(1,),
        flops=5 * 10**8,
        moved=5 * 2**20,
    )(
        part_low,
        part_high,
        next_low,
        next_high,
        gain_lap,
        gain_lap,
        forward_snaps,
        forward_snaps,
        omega_z,
        omega_x,
        omega_y,
        pool,
        sketch_mid,
    )
    got_edge = lax.all_to_all(chunks_edge, "shot", 0, 0, tiled=True)

    def layers_of(chunks, count):
        folded = chunks.reshape(count, half_x // part, shots, part, cells_y)
        return folded.transpose(2, 0, 1, 3, 4).reshape(shots, count, half_x, cells_y)

    edges = layers_of(chunks_edge, 2 * REACH)
    coarse = jnp.concatenate(
        [edges[:, :REACH], layers_of(chunks_mid, inner), edges[:, REACH:]], axis=1
    ).reshape(shots, cells_z, half_x * cells_y)

    all_shots = groups * shots
    gram = run(
        gram_kernel,
        shape((all_shots, cells_y), F32),
        in_specs=[vmem, vmem],
        out_specs=vmem,
        flops=10**8,
        moved=2**20,
    )(
        got_mid.reshape(all_shots * part, cells_y),
        got_edge.reshape(all_shots * part, cells_y),
    )
    mine = lax.all_to_all(gram.reshape(groups, shots, cells_y), "shot", 0, 0, tiled=True).sum(0)
    terms = jnp.concatenate([sketch_part, mine], axis=0)
    sums = lax.all_to_all(
        jnp.broadcast_to(terms[None], (slabs,) + terms.shape), "slab", 0, 0, tiled=True
    ).sum(0)
    sketch = sums[:shots] * (1.0 / math.sqrt(total_z * cells_x * cells_y))
    group = lax.axis_index("shot")
    partner = jnp.remainder(group - 1 - jnp.arange(LAGS, dtype=jnp.int32), groups)
    wanted = (partner[:, None] * shots + jnp.arange(shots, dtype=jnp.int32)[None, :]).reshape(-1)
    picked = wanted[:, None] == jnp.arange(cells_y, dtype=jnp.int32)[None, :]
    band = jnp.sum(jnp.where(picked[None], sums[shots:, None, :], 0.0), axis=-1)
    gram_band = band.reshape(shots, LAGS, shots) * (
        1.0 / math.sqrt(total_z * cells_x * cells_y // 2)
    )
    return (sketch, coarse, gram_band)


def solution(mesh):
    return jax.shard_map(
        local,
        mesh=mesh,
        in_specs=(
            P("slab", None, None),
            P("shot", "slab", None, None),
            P("shot", "slab", None, None),
            P("shot", None, "slab", None, None),
            P("shot", None, None),
            P("shot", None),
            P("shot", None),
            P("shot", None),
            P(),
            P("slab", None),
            P(),
            P(),
        ),
        out_specs=(P("shot", None), P("shot", "slab", None), P("shot", None, None)),
        check_vma=False,
    )
```

```python
import functools
import math

import jax
import jax.numpy as jnp
import ml_dtypes
import numpy as np
from jax import lax
from jax.experimental import pallas as pl
from jax.experimental.pallas import tpu as pltpu
from jax.sharding import PartitionSpec as P

LAGS = 4
REACH = 4
WHOLE_TAPS = (None, 8064.0, -1008.0, 128.0, -9.0)
DIVISOR = 5040.0
CENTRE = 3.0 * (-205.0 / 72.0)
DAMP_PEAK = 0.3
F32 = jnp.float32
BF16 = jnp.bfloat16
VMEM_BYTES = 24 * 1024 * 1024


def band_matrix(cells):
    index = np.arange(cells)
    apart = np.abs(index[:, None] - index[None, :])
    band = np.zeros((cells, cells), np.float32)
    for offset in range(1, REACH + 1):
        band[apart == offset] = WHOLE_TAPS[offset]
    return band.astype(ml_dtypes.bfloat16)


def pool_matrix(cells_y):
    half = cells_y // 2
    pool = np.zeros((2 * cells_y, 2 * half), np.float32)
    index = np.arange(cells_y)
    pool[index, index // 2] = 0.5
    pool[cells_y + index, half + index // 2] = 0.5
    return pool.astype(ml_dtypes.bfloat16)


def dot(left, right):
    return lax.dot_general(left, right, (((1,), (0,)), ((), ())), preferred_element_type=F32)


def dot_rows(left, right):
    return lax.dot_general(left, right, (((1,), (1,)), ((), ())), preferred_element_type=F32)


def two_parts(values):
    high = values.astype(BF16)
    low = (values - high.astype(F32)).astype(BF16)
    return high, low


def along_xy(planes, band_y, band_x):
    parts = [two_parts(plane) for plane in planes]
    rows = [jnp.concatenate(pair, axis=1) for pair in parts]
    columns = [jnp.concatenate(pair, axis=0) for pair in parts]
    over_y = dot(jnp.concatenate(rows, axis=0), band_y[...])
    over_x = dot(band_x[...], jnp.concatenate(columns, axis=1))
    cells_x, cells_y = planes[0].shape
    return [
        over_y[shot * cells_x : (shot + 1) * cells_x] + over_x[:, shot * cells_y : (shot + 1) * cells_y]
        for shot in range(len(planes))
    ]


def along_z(field, shot, z, cells_z):
    total = None
    for offset in range(1, REACH + 1):
        tap = WHOLE_TAPS[offset]
        below = jnp.where(z - offset >= 0, tap, 0.0)
        above = jnp.where(z + offset < cells_z, tap, 0.0)
        term = below * field[shot, jnp.maximum(z - offset, 0)]
        term += above * field[shot, jnp.minimum(z + offset, cells_z - 1)]
        total = term if total is None else total + term
    return total


def ramp_squared(index, length, thickness):
    distance = jnp.minimum(index, length - 1 - index).astype(F32)
    reach = jnp.full(index.shape, thickness, jnp.int32).astype(F32)
    ramp = jnp.maximum((reach - distance) / reach, 0.0)
    return ramp * ramp


def fetch(pairs, sems):
    copies = [
        pltpu.make_async_copy(source, target, sems.at[index])
        for index, (source, target) in enumerate(pairs)
    ]
    for copy in copies:
        copy.start()
    return copies


def begin_kernel(
    total_z,
    blocks,
    pml,
    curr,
    courant_hbm,
    prev_hbm,
    traces_hbm,
    place_z_hbm,
    place_x_hbm,
    place_y_hbm,
    band_y_hbm,
    band_x_hbm,
    updated,
    rest,
    gain_self,
    gain_lap,
    courant,
    prev,
    traces,
    place_z,
    place_x,
    place_y,
    band_y,
    band_x,
    ramp_z,
    ramp_xy,
    inject,
    sems,
):
    cells_z, cells_x, cells_y = courant.shape
    shots = curr.shape[0]
    step = cells_z // blocks
    pairs = [
        (traces_hbm, traces),
        (place_z_hbm, place_z),
        (place_x_hbm, place_x),
        (place_y_hbm, place_y),
        (band_y_hbm, band_y),
        (band_x_hbm, band_x),
    ]
    few = len(pairs)
    for block in range(blocks):
        span = pl.ds(block * step, step)
        pairs.append((courant_hbm.at[span], courant.at[span]))
        pairs.append((prev_hbm.at[:, span], prev.at[:, span]))
    copies = fetch(pairs, sems)
    first_z = lax.axis_index("slab") * cells_z
    plane = (cells_x, cells_y)
    row = lax.broadcasted_iota(jnp.int32, plane, 0)
    column = lax.broadcasted_iota(jnp.int32, plane, 1)
    ramp_z[...] = ramp_squared(
        lax.broadcasted_iota(jnp.int32, ramp_z.shape, 0) + first_z, total_z, pml[0]
    )
    ramp_xy[...] = ramp_squared(row, cells_x, pml[1]) + ramp_squared(column, cells_y, pml[2])
    for copy in copies[:few]:
        copy.wait()
    receivers = traces.shape[2]
    cell = lax.broadcasted_iota(jnp.int32, (cells_y, receivers), 0)
    for shot in range(shots):
        here = cell == place_y[shot : shot + 1, :]
        for instant in range(2):
            high, low = two_parts(jnp.where(here, traces[shot, instant : instant + 1, :], 0.0))
            span = slice(instant * cells_y, (instant + 1) * cells_y)
            inject[shot, span, :receivers] = high
            inject[shot, span, receivers:] = low
    line = lax.broadcasted_iota(jnp.int32, (cells_x, receivers), 0)

    def one_layer(z):
        damping = DAMP_PEAK * (ramp_z[pl.ds(z, 1), :] + ramp_xy[...])
        scale = 1.0 / (1.0 + damping)
        speed = courant[z]
        lap_gain = scale * (speed * speed)
        self_gain = 2.0 * scale + CENTRE * lap_gain
        lap_gain = lap_gain * (1.0 / DIVISOR)
        prev_gain = scale * (1.0 - damping)
        gain_self[z] = self_gain
        gain_lap[z] = lap_gain
        laps = along_xy([curr[shot, z] for shot in range(shots)], band_y, band_x)
        for shot in range(shots):
            now = curr[shot, z]
            lap = laps[shot] + along_z(curr, shot, z, cells_z)
            code = (place_z[shot : shot + 1, :] - first_z - z) * cells_x + place_x[shot : shot + 1, :]
            mark = jnp.where(line == code, 1.0, 0.0).astype(BF16)
            source = dot_rows(jnp.concatenate([mark, mark], axis=1), inject[shot])
            updated[shot, z] = (
                self_gain * now
                - prev_gain * prev[shot, z]
                + lap_gain * lap
                + scale * source[:, :cells_y]
            )
            rest[shot, z] = scale * source[:, cells_y:] - prev_gain * now

    for block in range(blocks):
        for copy in copies[few + 2 * block : few + 2 * block + 2]:
            copy.wait()
        pl.loop(block * step, (block + 1) * step)(one_layer)


def halo_terms(halo, shot, layer, upper):
    total = None
    for offset in range(1, REACH + 1):
        at = layer + offset - REACH if upper else layer - offset + REACH
        if 0 <= at < REACH:
            term = WHOLE_TAPS[offset] * halo[shot, at]
            total = term if total is None else total + term
    return total


def edge_kernel(upper, partial, halo, gain_lap, whole, out):
    @pl.loop(0, partial.shape[0])
    def _(shot):
        for layer in range(REACH):
            value = partial[shot, layer] + gain_lap[layer] * halo_terms(halo, shot, layer, upper)
            whole[shot, layer] = value
            out[shot, layer] = value


def emit(gradients, layer, spread_y, weight_z, pool, chunks, total, lines):
    shots = len(gradients)
    rounded = [gradient.astype(BF16) for gradient in gradients]
    cells_x = rounded[0].shape[0]
    spread = dot(jnp.concatenate(rounded, axis=0), spread_y[...])
    half = cells_x // 2
    pairs = []
    for shot in range(shots):
        total[shot] += spread[shot * cells_x : (shot + 1) * cells_x] * weight_z
        lines[shot] = rounded[shot].astype(F32)
        even = lines[shot, pl.ds(0, half, stride=2), :].astype(BF16)
        odd = lines[shot, pl.ds(1, half, stride=2), :].astype(BF16)
        pairs.append(jnp.concatenate([even, odd], axis=1))
    coarse = dot(jnp.concatenate(pairs, axis=0), pool[...])
    part = chunks.shape[2]
    pieces = half // part
    for shot in range(shots):
        for piece in range(pieces):
            start = shot * half + piece * part
            chunks[layer * pieces + piece, shot] = coarse[start : start + part]


def middle_kernel(
    blocks,
    wave,
    rest,
    gain_self,
    gain_lap,
    snaps_hbm,
    omega_z_hbm,
    omega_x_hbm,
    omega_y_hbm,
    band_y_hbm,
    band_x_hbm,
    pool_hbm,
    panels,
    edges,
    edge_gain,
    sketch,
    snaps,
    omega_z,
    omega_x,
    omega_y,
    band_y,
    band_x,
    pool,
    total,
    spread_y,
    lines,
    chunks,
    sems,
):
    shots, cells_z = wave.shape[:2]
    last = cells_z - REACH
    step = cells_z // blocks
    pairs = [
        (band_y_hbm, band_y),
        (band_x_hbm, band_x),
        (omega_y_hbm, omega_y),
        (omega_z_hbm, omega_z),
        (pool_hbm, pool),
        (omega_x_hbm, omega_x),
    ]
    few = len(pairs)
    order = list(range(1, blocks - 1)) + [0, blocks - 1]
    for block in order:
        span = pl.ds(block * step, step)
        pairs.append((snaps_hbm.at[:, :, span], snaps.at[:, :, span]))
    copies = fetch(pairs, sems)
    total[...] = jnp.zeros_like(total)
    for copy in copies[:few]:
        copy.wait()
    spread_y[...] = omega_y[...].astype(F32).astype(BF16)

    def gradients_at(z):
        laps = along_xy([wave[shot, z] for shot in range(shots)], band_y, band_x)
        gradients = []
        for shot in range(shots):
            lap = laps[shot] + along_z(wave, shot, z, cells_z)
            now = wave[shot, z]
            later = gain_self[z] * now + rest[shot, z] + gain_lap[z] * lap
            gradients.append(
                now * snaps[shot, 0, z].astype(F32) + later * snaps[shot, 1, z].astype(F32)
            )
        return gradients

    def middle_layer(z):
        weight_z = omega_z[pl.ds(z, 1), :].astype(F32)
        emit(gradients_at(z), z - REACH, spread_y, weight_z, pool, chunks, total, lines)

    def edge_layer(index):
        z = index + jnp.where(index >= REACH, last - REACH, 0)
        gradients = gradients_at(z)
        for shot in range(shots):
            edges[shot, index] = gradients[shot]
            edge_gain[shot, index] = gain_lap[z] * snaps[shot, 1, z].astype(F32)

    for place, block in enumerate(order[:-2]):
        copies[few + place].wait()
        pl.loop(block * step, (block + 1) * step)(middle_layer)
    send = pltpu.make_async_copy(
        chunks, panels.at[:, :, pl.ds(0, chunks.shape[2])], sems.at[len(pairs)]
    )
    send.start()
    for copy in copies[few + blocks - 2 :]:
        copy.wait()
    pl.loop(0, 2 * REACH)(edge_layer)
    weights_x = omega_x[...].astype(F32)
    for shot in range(shots):
        sketch[shot : shot + 1, :] = jnp.sum(total[shot] * weights_x, axis=0, keepdims=True)
    send.wait()


def finish_kernel(
    panels_before,
    edges,
    edge_gain,
    halo_low,
    halo_high,
    omega_z,
    omega_x,
    omega_y,
    pool,
    before,
    panels,
    sketch,
    total,
    spread_y,
    lines,
    chunks,
    sem,
):
    shots = edges.shape[0]
    cells_z = omega_z.shape[0]
    spread_y[...] = omega_y[...].astype(F32).astype(BF16)
    total[...] = jnp.zeros_like(total)
    for halo, upper in ((halo_low, False), (halo_high, True)):
        for layer in range(REACH):
            index = layer + (REACH if upper else 0)
            z = cells_z - REACH + layer if upper else layer
            gradients = [
                edges[shot, index]
                + edge_gain[shot, index] * halo_terms(halo, shot, layer, upper)
                for shot in range(shots)
            ]
            weight_z = omega_z[z : z + 1, :].astype(F32)
            emit(gradients, index, spread_y, weight_z, pool, chunks, total, lines)
    part = chunks.shape[2]
    send = pltpu.make_async_copy(chunks, panels.at[:, :, pl.ds(part, part)], sem.at[0])
    send.start()
    weights_x = omega_x[...].astype(F32)
    for shot in range(shots):
        sketch[shot : shot + 1, :] = before[shot : shot + 1, :] + jnp.sum(
            total[shot] * weights_x, axis=0, keepdims=True
        )
    send.wait()


def gram_kernel(panels, out):
    shots = out.shape[0]
    part = panels.shape[0] // shots
    width = 8
    gram = None
    for start in range(0, part, width):
        rows = [panels[pl.ds(start + index, shots, stride=part), :] for index in range(width)]
        high, low = two_parts(jnp.concatenate(rows, axis=1))
        both = jnp.concatenate([high, low], axis=0)
        term = dot_rows(both, both)
        gram = term if gram is None else gram + term
    folded = (gram[:shots, :shots] + gram[shots:, shots:]) + (
        gram[:shots, shots:] + gram[shots:, :shots]
    )
    out[...] = jnp.zeros_like(out)
    out[:, :shots] = folded


def spec(block=None, index=None):
    if block is None:
        return pl.BlockSpec(memory_space=pltpu.VMEM)
    return pl.BlockSpec(block, lambda step: index)


def run(kernel, out_shape, in_specs, out_specs, scratch=(), flops=0, moved=0, grid=None, **options):
    if grid is not None:
        options["grid"] = grid
    return pl.pallas_call(
        kernel,
        out_shape=out_shape,
        in_specs=in_specs,
        out_specs=out_specs,
        scratch_shapes=scratch,
        compiler_params=pltpu.CompilerParams(vmem_limit_bytes=VMEM_BYTES),
        cost_estimate=pl.CostEstimate(flops=flops, bytes_accessed=moved, transcendentals=0),
        **options,
    )


def local(
    courant,
    adj_prev,
    adj_curr,
    forward_snaps,
    traces,
    receiver_z,
    receiver_x,
    receiver_y,
    pml_cells,
    omega_z,
    omega_x,
    omega_y,
):
    shots, cells_z, cells_x, cells_y = adj_curr.shape
    slabs = lax.axis_size("slab")
    groups = lax.axis_size("shot")
    total_z = cells_z * slabs
    last = cells_z - REACH
    inner = last - REACH
    rank = omega_z.shape[1]
    receivers = traces.shape[2]
    half_x = cells_x // 2
    part = inner * half_x // groups
    blocks = cells_z // REACH
    shape = jax.ShapeDtypeStruct
    plane = (cells_x, cells_y)
    band = band_matrix(cells_y)
    band_y = jnp.asarray(np.concatenate([band, band], axis=0))
    band = band_matrix(cells_x)
    band_x = jnp.asarray(np.concatenate([band, band], axis=1))
    pool = jnp.asarray(pool_matrix(cells_y))

    def from_below(layers):
        return lax.ppermute(layers, "slab", [(i, i + 1) for i in range(slabs - 1)])

    def from_above(layers):
        return lax.ppermute(layers, "slab", [(i + 1, i) for i in range(slabs - 1)])

    halo_low = from_below(adj_curr[:, last:])
    halo_high = from_above(adj_curr[:, :REACH])

    vmem = spec()
    hbm = pl.BlockSpec(memory_space=pltpu.HBM)

    def pinned(*arrays):
        return [pltpu.with_memory_space_constraint(array, pltpu.HBM) for array in arrays]

    field = shape((shots, cells_z) + plane, F32)
    gain = shape((cells_z,) + plane, F32)
    edge = shape((shots, REACH) + plane, F32)
    like = lambda array: pltpu.VMEM(array.shape, array.dtype)
    updated, rest, gain_self, gain_lap = run(
        functools.partial(begin_kernel, total_z, blocks),
        [field, field, gain, gain],
        in_specs=[pl.BlockSpec(memory_space=pltpu.SMEM), vmem] + [hbm] * 8,
        out_specs=[vmem] * 4,
        scratch=[
            like(courant),
            like(adj_prev),
            like(traces),
            like(receiver_z),
            like(receiver_x),
            like(receiver_y),
            like(band_y),
            like(band_x),
            pltpu.VMEM((cells_z, cells_y), F32),
            pltpu.VMEM(plane, F32),
            pltpu.VMEM((shots, 2 * cells_y, 2 * receivers), BF16),
            pltpu.SemaphoreType.DMA((6 + 2 * blocks,)),
        ],
        flops=2 * 10**9,
        moved=11 * 2**20,
    )(
        pml_cells,
        adj_curr,
        *pinned(
            courant, adj_prev, traces, receiver_z, receiver_x, receiver_y, band_y, band_x
        ),
    )

    layers4 = (shots, REACH) + plane
    gains4 = (REACH,) + plane

    def complete(whole, halo, upper):
        side = blocks - 1 if upper else 0
        return run(
            functools.partial(edge_kernel, upper),
            [field, edge],
            in_specs=[
                spec(layers4, (0, side, 0, 0)),
                spec(layers4, (0, 0, 0, 0)),
                spec(gains4, (side, 0, 0)),
            ],
            out_specs=[spec(layers4, (0, side, 0, 0)), spec(layers4, (0, 0, 0, 0))],
            grid=(1,),
            flops=10**7,
            moved=2 * 2**20,
            input_output_aliases={0: 0},
        )(whole, halo, gain_lap)

    wave, edge_low = complete(updated, halo_low, False)
    wave, edge_high = complete(wave, halo_high, True)
    next_high = from_above(edge_low)
    next_low = from_below(edge_high)

    panel = shape((groups, shots, 2 * part, cells_y), F32)
    scratch_emit = [
        pltpu.VMEM((shots, cells_x, rank), F32),
        pltpu.VMEM((cells_y, rank), BF16),
        pltpu.VMEM((shots,) + plane, F32),
        pltpu.VMEM((groups, shots, part, cells_y), F32),
    ]
    both = shape((shots, 2 * REACH) + plane, F32)
    panels, edges, edge_gain, sketch_mid = run(
        functools.partial(middle_kernel, blocks),
        [panel, both, both, shape((shots, rank), F32)],
        in_specs=[vmem] * 4 + [hbm] * 7,
        out_specs=[hbm, vmem, vmem, vmem],
        scratch=[
            like(forward_snaps),
            like(omega_z),
            like(omega_x),
            like(omega_y),
            like(band_y),
            like(band_x),
            like(pool),
        ]
        + scratch_emit
        + [pltpu.SemaphoreType.DMA((7 + blocks,))],
        flops=2 * 10**9,
        moved=11 * 2**20,
    )(
        wave,
        rest,
        gain_self,
        gain_lap,
        *pinned(forward_snaps, omega_z, omega_x, omega_y, band_y, band_x, pool),
    )

    panels, sketch_part = run(
        finish_kernel,
        [panel, shape((shots, rank), F32)],
        in_specs=[hbm] + [vmem] * 9,
        out_specs=[hbm, vmem],
        scratch=scratch_emit + [pltpu.SemaphoreType.DMA((1,))],
        flops=5 * 10**8,
        moved=5 * 2**20,
        input_output_aliases={0: 0},
    )(
        panels,
        edges,
        edge_gain,
        next_low,
        next_high,
        omega_z,
        omega_x,
        omega_y,
        pool,
        sketch_mid,
    )
    got = lax.all_to_all(panels, "shot", 0, 0, tiled=True)

    folded = panels.reshape(inner, half_x // part, shots, 2, part, cells_y)
    folded = folded.transpose(3, 2, 0, 1, 4, 5).reshape(2, shots, inner, half_x, cells_y)
    coarse = jnp.concatenate(
        [folded[1, :, :REACH], folded[0], folded[1, :, REACH:]], axis=1
    ).reshape(shots, cells_z, half_x * cells_y)

    all_shots = groups * shots
    gram = run(
        gram_kernel,
        shape((all_shots, cells_y), F32),
        in_specs=[vmem],
        out_specs=vmem,
        flops=10**8,
        moved=2**20,
    )(got.reshape(all_shots * 2 * part, cells_y))
    mine = lax.all_to_all(gram.reshape(groups, shots, cells_y), "shot", 0, 0, tiled=True).sum(0)
    terms = jnp.concatenate([sketch_part, mine], axis=0)
    sums = lax.all_to_all(
        jnp.broadcast_to(terms[None], (slabs,) + terms.shape), "slab", 0, 0, tiled=True
    ).sum(0)
    sketch = sums[:shots] * (1.0 / math.sqrt(total_z * cells_x * cells_y))
    group = lax.axis_index("shot")
    partner = jnp.remainder(group - 1 - jnp.arange(LAGS, dtype=jnp.int32), groups)
    wanted = (partner[:, None] * shots + jnp.arange(shots, dtype=jnp.int32)[None, :]).reshape(-1)
    picked = wanted[:, None] == jnp.arange(cells_y, dtype=jnp.int32)[None, :]
    band = jnp.sum(jnp.where(picked[None], sums[shots:, None, :], 0.0), axis=-1)
    gram_band = band.reshape(shots, LAGS, shots) * (
        1.0 / math.sqrt(total_z * cells_x * cells_y // 2)
    )
    return (sketch, coarse, gram_band)


def solution(mesh):
    return jax.shard_map(
        local,
        mesh=mesh,
        in_specs=(
            P("slab", None, None),
            P("shot", "slab", None, None),
            P("shot", "slab", None, None),
            P("shot", None, "slab", None, None),
            P("shot", None, None),
            P("shot", None),
            P("shot", None),
            P("shot", None),
            P(),
            P("slab", None),
            P(),
            P(),
        ),
        out_specs=(P("shot", None), P("shot", "slab", None), P("shot", None, None)),
        check_vma=False,
    )
```

```python
import functools
import math

import jax
import jax.numpy as jnp
import ml_dtypes
import numpy as np
from jax import lax
from jax.experimental import pallas as pl
from jax.experimental.pallas import tpu as pltpu
from jax.sharding import PartitionSpec as P

LAGS = 4
REACH = 4
WHOLE_TAPS = (None, 8064.0, -1008.0, 128.0, -9.0)
DIVISOR = 5040.0
CENTRE = 3.0 * (-205.0 / 72.0)
DAMP_PEAK = 0.3
F32 = jnp.float32
BF16 = jnp.bfloat16
VMEM_BYTES = 24 * 1024 * 1024


def band_matrix(cells):
    index = np.arange(cells)
    apart = np.abs(index[:, None] - index[None, :])
    band = np.zeros((cells, cells), np.float32)
    for offset in range(1, REACH + 1):
        band[apart == offset] = WHOLE_TAPS[offset]
    return band.astype(ml_dtypes.bfloat16)


def pool_matrix(cells_y):
    half = cells_y // 2
    pool = np.zeros((2 * cells_y, 2 * half), np.float32)
    index = np.arange(cells_y)
    pool[index, index // 2] = 0.5
    pool[cells_y + index, half + index // 2] = 0.5
    return pool.astype(ml_dtypes.bfloat16)


def dot(left, right):
    return lax.dot_general(left, right, (((1,), (0,)), ((), ())), preferred_element_type=F32)


def dot_rows(left, right):
    return lax.dot_general(left, right, (((1,), (1,)), ((), ())), preferred_element_type=F32)


def two_parts(values):
    high = values.astype(BF16)
    low = (values - high.astype(F32)).astype(BF16)
    return high, low


def along_xy(planes, band_y, band_x):
    parts = [two_parts(plane) for plane in planes]
    rows = [jnp.concatenate(pair, axis=1) for pair in parts]
    columns = [jnp.concatenate(pair, axis=0) for pair in parts]
    over_y = dot(jnp.concatenate(rows, axis=0), band_y[...])
    over_x = dot(band_x[...], jnp.concatenate(columns, axis=1))
    cells_x, cells_y = planes[0].shape
    return [
        over_y[shot * cells_x : (shot + 1) * cells_x] + over_x[:, shot * cells_y : (shot + 1) * cells_y]
        for shot in range(len(planes))
    ]


def along_z(field, shot, z, cells_z):
    total = None
    for offset in range(1, REACH + 1):
        tap = WHOLE_TAPS[offset]
        below = jnp.where(z - offset >= 0, tap, 0.0)
        above = jnp.where(z + offset < cells_z, tap, 0.0)
        term = below * field[shot, jnp.maximum(z - offset, 0)]
        term += above * field[shot, jnp.minimum(z + offset, cells_z - 1)]
        total = term if total is None else total + term
    return total


def ramp_squared(index, length, thickness):
    distance = jnp.minimum(index, length - 1 - index).astype(F32)
    reach = jnp.full(index.shape, thickness, jnp.int32).astype(F32)
    ramp = jnp.maximum((reach - distance) / reach, 0.0)
    return ramp * ramp


def fetch(pairs, sems):
    copies = [
        pltpu.make_async_copy(source, target, sems.at[index])
        for index, (source, target) in enumerate(pairs)
    ]
    for copy in copies:
        copy.start()
    return copies


def begin_kernel(
    total_z,
    blocks,
    pml,
    curr,
    courant_hbm,
    prev_hbm,
    traces_hbm,
    place_z_hbm,
    place_x_hbm,
    place_y_hbm,
    band_y_hbm,
    band_x_hbm,
    updated,
    rest,
    gain_self,
    gain_lap,
    courant,
    prev,
    traces,
    place_z,
    place_x,
    place_y,
    band_y,
    band_x,
    ramp_z,
    ramp_xy,
    inject,
    sems,
):
    cells_z, cells_x, cells_y = courant.shape
    shots = curr.shape[0]
    step = cells_z // blocks
    pairs = [
        (traces_hbm, traces),
        (place_z_hbm, place_z),
        (place_x_hbm, place_x),
        (place_y_hbm, place_y),
        (band_y_hbm, band_y),
        (band_x_hbm, band_x),
    ]
    few = len(pairs)
    for block in range(blocks):
        span = pl.ds(block * step, step)
        pairs.append((courant_hbm.at[span], courant.at[span]))
        pairs.append((prev_hbm.at[:, span], prev.at[:, span]))
    copies = fetch(pairs, sems)
    first_z = lax.axis_index("slab") * cells_z
    plane = (cells_x, cells_y)
    row = lax.broadcasted_iota(jnp.int32, plane, 0)
    column = lax.broadcasted_iota(jnp.int32, plane, 1)
    ramp_z[...] = ramp_squared(
        lax.broadcasted_iota(jnp.int32, ramp_z.shape, 0) + first_z, total_z, pml[0]
    )
    ramp_xy[...] = ramp_squared(row, cells_x, pml[1]) + ramp_squared(column, cells_y, pml[2])
    for copy in copies[:few]:
        copy.wait()
    receivers = traces.shape[2]
    cell = lax.broadcasted_iota(jnp.int32, (cells_y, receivers), 0)
    for shot in range(shots):
        here = cell == place_y[shot : shot + 1, :]
        for instant in range(2):
            high, low = two_parts(jnp.where(here, traces[shot, instant : instant + 1, :], 0.0))
            span = slice(instant * cells_y, (instant + 1) * cells_y)
            inject[shot, span, :receivers] = high
            inject[shot, span, receivers:] = low
    line = lax.broadcasted_iota(jnp.int32, (cells_x, receivers), 0)

    def one_layer(z):
        damping = DAMP_PEAK * (ramp_z[pl.ds(z, 1), :] + ramp_xy[...])
        scale = 1.0 / (1.0 + damping)
        speed = courant[z]
        lap_gain = scale * (speed * speed)
        self_gain = 2.0 * scale + CENTRE * lap_gain
        lap_gain = lap_gain * (1.0 / DIVISOR)
        prev_gain = scale * (1.0 - damping)
        gain_self[z] = self_gain
        gain_lap[z] = lap_gain
        laps = along_xy([curr[shot, z] for shot in range(shots)], band_y, band_x)
        for shot in range(shots):
            now = curr[shot, z]
            lap = laps[shot] + along_z(curr, shot, z, cells_z)
            code = (place_z[shot : shot + 1, :] - first_z - z) * cells_x + place_x[shot : shot + 1, :]
            mark = jnp.where(line == code, 1.0, 0.0).astype(BF16)
            source = dot_rows(jnp.concatenate([mark, mark], axis=1), inject[shot])
            updated[shot, z] = (
                self_gain * now
                - prev_gain * prev[shot, z]
                + lap_gain * lap
                + scale * source[:, :cells_y]
            )
            rest[shot, z] = scale * source[:, cells_y:] - prev_gain * now

    for block in range(blocks):
        for copy in copies[few + 2 * block : few + 2 * block + 2]:
            copy.wait()
        pl.loop(block * step, (block + 1) * step)(one_layer)


def odd_slab():
    return lax.rem(lax.axis_index("slab"), 2)


def slice_kernel(curr, near, far, sems):
    layers = near.shape[1]
    last = curr.shape[1] - layers
    odd = odd_slab()
    copies = fetch(
        [
            (curr.at[:, pl.ds((1 - odd) * last, layers)], near),
            (curr.at[:, pl.ds(odd * last, layers)], far),
        ],
        sems,
    )
    for copy in copies:
        copy.wait()


def halo_terms(halo, layer, upper):
    total = None
    for offset in range(1, REACH + 1):
        at = layer + offset - REACH if upper else layer - offset + REACH
        if 0 <= at < REACH:
            term = WHOLE_TAPS[offset] * halo(at)
            total = term if total is None else total + term
    return total


def edge_kernel(partial, near, far, gain_lap, whole, near_out, far_out):
    odd = odd_slab()
    step = pl.program_id(0)
    for upper in (False, True):
        for halo, out, parity in (
            (near, near_out, 0 if upper else 1),
            (far, far_out, 1 if upper else 0),
        ):

            @pl.when((step == int(upper)) & (odd == parity))
            def _():
                @pl.loop(0, partial.shape[0])
                def _(shot):
                    for layer in range(REACH):
                        terms = halo_terms(lambda at: halo[shot, at], layer, upper)
                        value = partial[shot, layer] + gain_lap[layer] * terms
                        whole[shot, layer] = value
                        out[shot, layer] = value


def emit(gradients, layer, spread_y, weight_z, pool, chunks, total, lines):
    shots = len(gradients)
    rounded = [gradient.astype(BF16) for gradient in gradients]
    cells_x = rounded[0].shape[0]
    spread = dot(jnp.concatenate(rounded, axis=0), spread_y[...])
    half = cells_x // 2
    pairs = []
    for shot in range(shots):
        total[shot] += spread[shot * cells_x : (shot + 1) * cells_x] * weight_z
        lines[shot] = rounded[shot].astype(F32)
        even = lines[shot, pl.ds(0, half, stride=2), :].astype(BF16)
        odd = lines[shot, pl.ds(1, half, stride=2), :].astype(BF16)
        pairs.append(jnp.concatenate([even, odd], axis=1))
    coarse = dot(jnp.concatenate(pairs, axis=0), pool[...])
    part = chunks.shape[2]
    pieces = half // part
    for shot in range(shots):
        for piece in range(pieces):
            start = shot * half + piece * part
            chunks[layer * pieces + piece, shot] = coarse[start : start + part]


def middle_kernel(
    blocks,
    wave,
    rest,
    gain_self,
    gain_lap,
    snaps_hbm,
    omega_z_hbm,
    omega_x_hbm,
    omega_y_hbm,
    band_y_hbm,
    band_x_hbm,
    pool_hbm,
    panels,
    edges,
    edge_gain,
    sketch,
    snaps,
    omega_z,
    omega_x,
    omega_y,
    band_y,
    band_x,
    pool,
    total,
    spread_y,
    lines,
    chunks,
    sems,
):
    shots, cells_z = wave.shape[:2]
    last = cells_z - REACH
    step = cells_z // blocks
    pairs = [
        (band_y_hbm, band_y),
        (band_x_hbm, band_x),
        (omega_y_hbm, omega_y),
        (omega_z_hbm, omega_z),
        (pool_hbm, pool),
        (omega_x_hbm, omega_x),
    ]
    few = len(pairs)
    order = list(range(1, blocks - 1)) + [0, blocks - 1]
    for block in order:
        span = pl.ds(block * step, step)
        pairs.append((snaps_hbm.at[:, :, span], snaps.at[:, :, span]))
    copies = fetch(pairs, sems)
    total[...] = jnp.zeros_like(total)
    for copy in copies[:few]:
        copy.wait()
    spread_y[...] = omega_y[...].astype(F32).astype(BF16)

    def gradients_at(z):
        laps = along_xy([wave[shot, z] for shot in range(shots)], band_y, band_x)
        gradients = []
        for shot in range(shots):
            lap = laps[shot] + along_z(wave, shot, z, cells_z)
            now = wave[shot, z]
            later = gain_self[z] * now + rest[shot, z] + gain_lap[z] * lap
            gradients.append(
                now * snaps[shot, 0, z].astype(F32) + later * snaps[shot, 1, z].astype(F32)
            )
        return gradients

    def middle_layer(z):
        weight_z = omega_z[pl.ds(z, 1), :].astype(F32)
        emit(gradients_at(z), z - REACH, spread_y, weight_z, pool, chunks, total, lines)

    def edge_layer(index):
        z = index + jnp.where(index >= REACH, last - REACH, 0)
        gradients = gradients_at(z)
        for shot in range(shots):
            edges[shot, index] = gradients[shot]
            edge_gain[shot, index] = gain_lap[z] * snaps[shot, 1, z].astype(F32)

    for place, block in enumerate(order[:-2]):
        copies[few + place].wait()
        pl.loop(block * step, (block + 1) * step)(middle_layer)
    send = pltpu.make_async_copy(
        chunks, panels.at[:, :, pl.ds(0, chunks.shape[2])], sems.at[len(pairs)]
    )
    send.start()
    for copy in copies[few + blocks - 2 :]:
        copy.wait()
    pl.loop(0, 2 * REACH)(edge_layer)
    weights_x = omega_x[...].astype(F32)
    for shot in range(shots):
        sketch[shot : shot + 1, :] = jnp.sum(total[shot] * weights_x, axis=0, keepdims=True)
    send.wait()


def finish_kernel(
    panels_before,
    edges,
    edge_gain,
    near,
    far,
    omega_z,
    omega_x,
    omega_y,
    pool,
    before,
    panels,
    sketch,
    total,
    spread_y,
    lines,
    chunks,
    sem,
):
    shots = edges.shape[0]
    cells_z = omega_z.shape[0]
    spread_y[...] = omega_y[...].astype(F32).astype(BF16)
    total[...] = jnp.zeros_like(total)
    is_odd = odd_slab() == 1

    def halo(shot, upper):
        first, second = (far, near) if upper else (near, far)
        return lambda at: jnp.where(is_odd, first[shot, at], second[shot, at])

    for upper in (False, True):
        for layer in range(REACH):
            index = layer + (REACH if upper else 0)
            z = cells_z - REACH + layer if upper else layer
            gradients = [
                edges[shot, index]
                + edge_gain[shot, index] * halo_terms(halo(shot, upper), layer, upper)
                for shot in range(shots)
            ]
            weight_z = omega_z[z : z + 1, :].astype(F32)
            emit(gradients, index, spread_y, weight_z, pool, chunks, total, lines)
    part = chunks.shape[2]
    send = pltpu.make_async_copy(chunks, panels.at[:, :, pl.ds(part, part)], sem.at[0])
    send.start()
    weights_x = omega_x[...].astype(F32)
    for shot in range(shots):
        sketch[shot : shot + 1, :] = before[shot : shot + 1, :] + jnp.sum(
            total[shot] * weights_x, axis=0, keepdims=True
        )
    send.wait()


def gram_kernel(panels, coarse, out):
    del coarse
    shots = out.shape[0]
    part = panels.shape[0] // shots
    width = 8
    gram = None
    for start in range(0, part, width):
        rows = [panels[pl.ds(start + index, shots, stride=part), :] for index in range(width)]
        high, low = two_parts(jnp.concatenate(rows, axis=1))
        both = jnp.concatenate([high, low], axis=0)
        term = dot_rows(both, both)
        gram = term if gram is None else gram + term
    folded = (gram[:shots, :shots] + gram[shots:, shots:]) + (
        gram[:shots, shots:] + gram[shots:, :shots]
    )
    out[...] = jnp.zeros_like(out)
    out[:, :shots] = folded


def gather_kernel(mine, sketch, out):
    shots = sketch.shape[0]
    total = mine[0]
    for source in range(1, mine.shape[0]):
        total = total + mine[source]
    for target in range(out.shape[0]):
        out[target, :shots] = sketch[...]
        out[target, shots:] = total


def output_kernel(
    groups, sketch_scale, gram_scale, terms, sketch_hbm, gram_hbm, sketch, gram_band, sems
):
    shots, _, lags = gram_band.shape
    lanes = terms.shape[2]
    total = terms[0]
    for source in range(1, terms.shape[0]):
        total = total + terms[source]
    sketch[...] = total[:shots] * sketch_scale
    group = lax.axis_index("shot")
    lag = lax.broadcasted_iota(jnp.int32, (lags, lanes), 0)
    lane = lax.broadcasted_iota(jnp.int32, (lags, lanes), 1)
    partner = group - 1 - lag
    partner = jnp.where(partner < 0, partner + groups, partner)
    for shot in range(shots):
        row = total[shots + shot : shots + shot + 1] * gram_scale
        for other in range(shots):
            wanted = lane == partner * shots + other
            picked = jnp.sum(jnp.where(wanted, row, 0.0), axis=1, keepdims=True)
            turned = jnp.sum(jnp.where(lane == lag, picked, 0.0), axis=0, keepdims=True)
            gram_band[shot, other : other + 1, :] = turned[:, :lags]
    for copy in fetch([(sketch, sketch_hbm), (gram_band, gram_hbm)], sems):
        copy.wait()


def spec(block=None, index=None):
    if block is None:
        return pl.BlockSpec(memory_space=pltpu.VMEM)
    return pl.BlockSpec(block, lambda step: index)


def run(kernel, out_shape, in_specs, out_specs, scratch=(), flops=0, moved=0, grid=None, **options):
    if grid is not None:
        options["grid"] = grid
    return pl.pallas_call(
        kernel,
        out_shape=out_shape,
        in_specs=in_specs,
        out_specs=out_specs,
        scratch_shapes=scratch,
        compiler_params=pltpu.CompilerParams(vmem_limit_bytes=VMEM_BYTES),
        cost_estimate=pl.CostEstimate(flops=flops, bytes_accessed=moved, transcendentals=0),
        **options,
    )


def local(
    courant,
    adj_prev,
    adj_curr,
    forward_snaps,
    traces,
    receiver_z,
    receiver_x,
    receiver_y,
    pml_cells,
    omega_z,
    omega_x,
    omega_y,
):
    shots, cells_z, cells_x, cells_y = adj_curr.shape
    slabs = lax.axis_size("slab")
    groups = lax.axis_size("shot")
    total_z = cells_z * slabs
    last = cells_z - REACH
    inner = last - REACH
    rank = omega_z.shape[1]
    receivers = traces.shape[2]
    half_x = cells_x // 2
    part = inner * half_x // groups
    blocks = cells_z // REACH
    shape = jax.ShapeDtypeStruct
    plane = (cells_x, cells_y)
    band = band_matrix(cells_y)
    band_y = jnp.asarray(np.concatenate([band, band], axis=0))
    band = band_matrix(cells_x)
    band_x = jnp.asarray(np.concatenate([band, band], axis=1))
    pool = jnp.asarray(pool_matrix(cells_y))

    def with_near(layers):
        return lax.ppermute(layers, "slab", [(i, i ^ 1) for i in range(slabs)])

    def with_far(layers):
        pairs = [(i, i + 1) for i in range(1, slabs - 1, 2)]
        return lax.ppermute(layers, "slab", pairs + [(j, i) for i, j in pairs])

    vmem = spec()
    hbm = pl.BlockSpec(memory_space=pltpu.HBM)

    def pinned(*arrays):
        return [pltpu.with_memory_space_constraint(array, pltpu.HBM) for array in arrays]

    field = shape((shots, cells_z) + plane, F32)
    gain = shape((cells_z,) + plane, F32)
    edge = shape((shots, REACH) + plane, F32)
    like = lambda array: pltpu.VMEM(array.shape, array.dtype)
    near, far = run(
        slice_kernel,
        [edge, edge],
        in_specs=[hbm],
        out_specs=[vmem, vmem],
        scratch=[pltpu.SemaphoreType.DMA((2,))],
        moved=2**21,
    )(*pinned(adj_curr))
    far = with_far(far)
    near = with_near(near)
    updated, rest, gain_self, gain_lap = run(
        functools.partial(begin_kernel, total_z, blocks),
        [field, field, gain, gain],
        in_specs=[pl.BlockSpec(memory_space=pltpu.SMEM), vmem] + [hbm] * 8,
        out_specs=[vmem] * 4,
        scratch=[
            like(courant),
            like(adj_prev),
            like(traces),
            like(receiver_z),
            like(receiver_x),
            like(receiver_y),
            like(band_y),
            like(band_x),
            pltpu.VMEM((cells_z, cells_y), F32),
            pltpu.VMEM(plane, F32),
            pltpu.VMEM((shots, 2 * cells_y, 2 * receivers), BF16),
            pltpu.SemaphoreType.DMA((6 + 2 * blocks,)),
        ],
        flops=2 * 10**9,
        moved=11 * 2**20,
    )(
        pml_cells,
        adj_curr,
        *pinned(
            courant, adj_prev, traces, receiver_z, receiver_x, receiver_y, band_y, band_x
        ),
    )

    layers4 = (shots, REACH) + plane
    gains4 = (REACH,) + plane

    whole4 = spec(layers4, (0, 0, 0, 0))
    wave4 = pl.BlockSpec(layers4, lambda step: (0, step * (blocks - 1), 0, 0))
    wave, near, far = run(
        edge_kernel,
        [field, edge, edge],
        in_specs=[
            wave4,
            whole4,
            whole4,
            pl.BlockSpec(gains4, lambda step: (step * (blocks - 1), 0, 0)),
        ],
        out_specs=[wave4, whole4, whole4],
        grid=(2,),
        flops=10**7,
        moved=2 * 2**20,
        input_output_aliases={0: 0},
    )(updated, near, far, gain_lap)
    far = with_far(far)
    near = with_near(near)

    panel = shape((groups, shots, 2 * part, cells_y), F32)
    scratch_emit = [
        pltpu.VMEM((shots, cells_x, rank), F32),
        pltpu.VMEM((cells_y, rank), BF16),
        pltpu.VMEM((shots,) + plane, F32),
        pltpu.VMEM((groups, shots, part, cells_y), F32),
    ]
    both = shape((shots, 2 * REACH) + plane, F32)
    panels, edges, edge_gain, sketch_mid = run(
        functools.partial(middle_kernel, blocks),
        [panel, both, both, shape((shots, rank), F32)],
        in_specs=[vmem] * 4 + [hbm] * 7,
        out_specs=[hbm, vmem, vmem, vmem],
        scratch=[
            like(forward_snaps),
            like(omega_z),
            like(omega_x),
            like(omega_y),
            like(band_y),
            like(band_x),
            like(pool),
        ]
        + scratch_emit
        + [pltpu.SemaphoreType.DMA((7 + blocks,))],
        flops=2 * 10**9,
        moved=11 * 2**20,
    )(
        wave,
        rest,
        gain_self,
        gain_lap,
        *pinned(forward_snaps, omega_z, omega_x, omega_y, band_y, band_x, pool),
    )

    panels, sketch_part = run(
        finish_kernel,
        [panel, shape((shots, rank), F32)],
        in_specs=[hbm] + [vmem] * 9,
        out_specs=[hbm, vmem],
        scratch=scratch_emit + [pltpu.SemaphoreType.DMA((1,))],
        flops=5 * 10**8,
        moved=5 * 2**20,
        input_output_aliases={0: 0},
    )(
        panels,
        edges,
        edge_gain,
        near,
        far,
        omega_z,
        omega_x,
        omega_y,
        pool,
        sketch_mid,
    )
    got = lax.all_to_all(panels, "shot", 0, 0, tiled=True)

    folded = panels.reshape(inner, half_x // part, shots, 2, part, cells_y)
    folded = folded.transpose(3, 2, 0, 1, 4, 5).reshape(2, shots, inner, half_x, cells_y)
    coarse = jnp.concatenate(
        [folded[1, :, :REACH], folded[0], folded[1, :, REACH:]], axis=1
    ).reshape(shots, cells_z, half_x * cells_y)

    all_shots = groups * shots
    gram = run(
        gram_kernel,
        shape((all_shots, cells_y), F32),
        in_specs=[vmem, hbm],
        out_specs=vmem,
        flops=10**8,
        moved=2**20,
    )(got.reshape(all_shots * 2 * part, cells_y), *pinned(coarse))
    mine = lax.all_to_all(gram.reshape(groups, shots, cells_y), "shot", 0, 0, tiled=True)
    terms = run(
        gather_kernel,
        shape((slabs, 2 * shots, rank), F32),
        in_specs=[vmem, vmem],
        out_specs=vmem,
        moved=2**16,
    )(mine, sketch_part)
    terms = lax.all_to_all(terms, "slab", 0, 0, tiled=True)
    sketch, gram_band = run(
        functools.partial(
            output_kernel,
            groups,
            1.0 / math.sqrt(total_z * cells_x * cells_y),
            1.0 / math.sqrt(total_z * cells_x * cells_y // 2),
        ),
        [shape((shots, rank), F32), shape((shots, shots, LAGS), F32)],
        in_specs=[vmem],
        out_specs=[hbm, hbm],
        scratch=[
            pltpu.VMEM((shots, rank), F32),
            pltpu.VMEM((shots, shots, LAGS), F32),
            pltpu.SemaphoreType.DMA((2,)),
        ],
        moved=2**16,
    )(terms)
    return (sketch, coarse, gram_band.transpose(0, 2, 1))


def solution(mesh):
    return jax.shard_map(
        local,
        mesh=mesh,
        in_specs=(
            P("slab", None, None),
            P("shot", "slab", None, None),
            P("shot", "slab", None, None),
            P("shot", None, "slab", None, None),
            P("shot", None, None),
            P("shot", None),
            P("shot", None),
            P("shot", None),
            P(),
            P("slab", None),
            P(),
            P(),
        ),
        out_specs=(P("shot", None), P("shot", "slab", None), P("shot", None, None)),
        check_vma=False,
    )
```

```python
import functools
import math

import jax
import jax.numpy as jnp
import ml_dtypes
import numpy as np
from jax import lax
from jax.experimental import pallas as pl
from jax.experimental.pallas import tpu as pltpu
from jax.sharding import PartitionSpec as P

LAGS = 4
REACH = 4
WHOLE_TAPS = (None, 8064.0, -1008.0, 128.0, -9.0)
DIVISOR = 5040.0
CENTRE = 3.0 * (-205.0 / 72.0)
DAMP_PEAK = 0.3
F32 = jnp.float32
BF16 = jnp.bfloat16
VMEM_BYTES = 24 * 1024 * 1024


def band_matrix(cells):
    index = np.arange(cells)
    apart = np.abs(index[:, None] - index[None, :])
    band = np.zeros((cells, cells), np.float32)
    for offset in range(1, REACH + 1):
        band[apart == offset] = WHOLE_TAPS[offset]
    return band.astype(ml_dtypes.bfloat16)


def pool_matrix(cells_y):
    half = cells_y // 2
    pool = np.zeros((2 * cells_y, 2 * half), np.float32)
    index = np.arange(cells_y)
    pool[index, index // 2] = 0.5
    pool[cells_y + index, half + index // 2] = 0.5
    return pool.astype(ml_dtypes.bfloat16)


def dot(left, right):
    return lax.dot_general(left, right, (((1,), (0,)), ((), ())), preferred_element_type=F32)


def dot_rows(left, right):
    return lax.dot_general(left, right, (((1,), (1,)), ((), ())), preferred_element_type=F32)


def two_parts(values):
    high = values.astype(BF16)
    low = (values - high.astype(F32)).astype(BF16)
    return high, low


def along_xy(planes, band_y, band_x):
    parts = [two_parts(plane) for plane in planes]
    rows = [jnp.concatenate(pair, axis=1) for pair in parts]
    columns = [jnp.concatenate(pair, axis=0) for pair in parts]
    over_y = dot(jnp.concatenate(rows, axis=0), band_y[...])
    over_x = dot(band_x[...], jnp.concatenate(columns, axis=1))
    cells_x, cells_y = planes[0].shape
    return [
        over_y[shot * cells_x : (shot + 1) * cells_x] + over_x[:, shot * cells_y : (shot + 1) * cells_y]
        for shot in range(len(planes))
    ]


def along_z(field, shot, z, cells_z):
    total = None
    for offset in range(1, REACH + 1):
        tap = WHOLE_TAPS[offset]
        below = jnp.where(z - offset >= 0, tap, 0.0)
        above = jnp.where(z + offset < cells_z, tap, 0.0)
        term = below * field[shot, jnp.maximum(z - offset, 0)]
        term += above * field[shot, jnp.minimum(z + offset, cells_z - 1)]
        total = term if total is None else total + term
    return total


def ramp_squared(index, length, thickness):
    distance = jnp.minimum(index, length - 1 - index).astype(F32)
    reach = jnp.full(index.shape, thickness, jnp.int32).astype(F32)
    ramp = jnp.maximum((reach - distance) / reach, 0.0)
    return ramp * ramp


def fetch(pairs, sems):
    copies = [
        pltpu.make_async_copy(source, target, sems.at[index])
        for index, (source, target) in enumerate(pairs)
    ]
    for copy in copies:
        copy.start()
    return copies


def begin_kernel(
    total_z,
    blocks,
    pml,
    curr_hbm,
    courant_hbm,
    prev_hbm,
    traces_hbm,
    place_z_hbm,
    place_x_hbm,
    place_y_hbm,
    band_y_hbm,
    band_x_hbm,
    updated,
    rest,
    gain_self,
    gain_lap,
    curr,
    courant,
    prev,
    traces,
    place_z,
    place_x,
    place_y,
    band_y,
    band_x,
    ramp_z,
    ramp_xy,
    inject,
    sems,
):
    cells_z, cells_x, cells_y = courant.shape
    shots = curr.shape[0]
    step = cells_z // blocks
    pairs = [
        (traces_hbm, traces),
        (place_z_hbm, place_z),
        (place_x_hbm, place_x),
        (place_y_hbm, place_y),
        (band_y_hbm, band_y),
        (band_x_hbm, band_x),
    ]
    few = len(pairs)
    for block in range(blocks):
        span = pl.ds(block * step, step)
        pairs.append((curr_hbm.at[:, span], curr.at[:, span]))
        pairs.append((courant_hbm.at[span], courant.at[span]))
        pairs.append((prev_hbm.at[:, span], prev.at[:, span]))
    copies = fetch(pairs, sems)
    first_z = lax.axis_index("slab") * cells_z
    plane = (cells_x, cells_y)
    row = lax.broadcasted_iota(jnp.int32, plane, 0)
    column = lax.broadcasted_iota(jnp.int32, plane, 1)
    ramp_z[...] = ramp_squared(
        lax.broadcasted_iota(jnp.int32, ramp_z.shape, 0) + first_z, total_z, pml[0]
    )
    ramp_xy[...] = ramp_squared(row, cells_x, pml[1]) + ramp_squared(column, cells_y, pml[2])
    for copy in copies[:few]:
        copy.wait()
    receivers = traces.shape[2]
    cell = lax.broadcasted_iota(jnp.int32, (cells_y, receivers), 0)
    for shot in range(shots):
        here = cell == place_y[shot : shot + 1, :]
        for instant in range(2):
            high, low = two_parts(jnp.where(here, traces[shot, instant : instant + 1, :], 0.0))
            span = slice(instant * cells_y, (instant + 1) * cells_y)
            inject[shot, span, :receivers] = high
            inject[shot, span, receivers:] = low
    line = lax.broadcasted_iota(jnp.int32, (cells_x, receivers), 0)

    def one_layer(z):
        damping = DAMP_PEAK * (ramp_z[pl.ds(z, 1), :] + ramp_xy[...])
        scale = 1.0 / (1.0 + damping)
        speed = courant[z]
        lap_gain = scale * (speed * speed)
        self_gain = 2.0 * scale + CENTRE * lap_gain
        lap_gain = lap_gain * (1.0 / DIVISOR)
        prev_gain = scale * (1.0 - damping)
        gain_self[z] = self_gain
        gain_lap[z] = lap_gain
        laps = along_xy([curr[shot, z] for shot in range(shots)], band_y, band_x)
        for shot in range(shots):
            now = curr[shot, z]
            lap = laps[shot] + along_z(curr, shot, z, cells_z)
            code = (place_z[shot : shot + 1, :] - first_z - z) * cells_x + place_x[shot : shot + 1, :]
            mark = jnp.where(line == code, 1.0, 0.0).astype(BF16)
            source = dot_rows(jnp.concatenate([mark, mark], axis=1), inject[shot])
            updated[shot, z] = (
                self_gain * now
                - prev_gain * prev[shot, z]
                + lap_gain * lap
                + scale * source[:, :cells_y]
            )
            rest[shot, z] = scale * source[:, cells_y:] - prev_gain * now

    copies[few].wait()
    for block in range(blocks):
        if block + 1 < blocks:
            copies[few + 3 * block + 3].wait()
        for copy in copies[few + 3 * block + 1 : few + 3 * block + 3]:
            copy.wait()
        pl.loop(block * step, (block + 1) * step)(one_layer)


def odd_slab():
    return lax.rem(lax.axis_index("slab"), 2)


def slice_kernel(curr, near, far, sems):
    layers = near.shape[1]
    last = curr.shape[1] - layers
    odd = odd_slab()
    copies = fetch(
        [
            (curr.at[:, pl.ds((1 - odd) * last, layers)], near),
            (curr.at[:, pl.ds(odd * last, layers)], far),
        ],
        sems,
    )
    for copy in copies:
        copy.wait()


def halo_terms(halo, layer, upper):
    total = None
    for offset in range(1, REACH + 1):
        at = layer + offset - REACH if upper else layer - offset + REACH
        if 0 <= at < REACH:
            term = WHOLE_TAPS[offset] * halo(at)
            total = term if total is None else total + term
    return total


def edge_kernel(partial, near, far, gain_lap, whole, near_out, far_out):
    odd = odd_slab()
    step = pl.program_id(0)
    for upper in (False, True):
        for halo, out, parity in (
            (near, near_out, 0 if upper else 1),
            (far, far_out, 1 if upper else 0),
        ):

            @pl.when((step == int(upper)) & (odd == parity))
            def _():
                @pl.loop(0, partial.shape[0])
                def _(shot):
                    for layer in range(REACH):
                        terms = halo_terms(lambda at: halo[shot, at], layer, upper)
                        value = partial[shot, layer] + gain_lap[layer] * terms
                        whole[shot, layer] = value
                        out[shot, layer] = value


def emit(gradients, layer, spread_y, weight_z, pool, chunks, total, lines):
    shots = len(gradients)
    rounded = [gradient.astype(BF16) for gradient in gradients]
    cells_x = rounded[0].shape[0]
    spread = dot(jnp.concatenate(rounded, axis=0), spread_y[...])
    half = cells_x // 2
    pairs = []
    for shot in range(shots):
        total[shot] += spread[shot * cells_x : (shot + 1) * cells_x] * weight_z
        lines[shot] = rounded[shot].astype(F32)
        even = lines[shot, pl.ds(0, half, stride=2), :].astype(BF16)
        odd = lines[shot, pl.ds(1, half, stride=2), :].astype(BF16)
        pairs.append(jnp.concatenate([even, odd], axis=1))
    coarse = dot(jnp.concatenate(pairs, axis=0), pool[...])
    part = chunks.shape[2]
    pieces = half // part
    for shot in range(shots):
        for piece in range(pieces):
            start = shot * half + piece * part
            chunks[layer * pieces + piece, shot] = coarse[start : start + part]


def middle_kernel(
    blocks,
    wave,
    rest,
    gain_self,
    gain_lap,
    snaps_hbm,
    omega_z_hbm,
    omega_y_hbm,
    band_y_hbm,
    band_x_hbm,
    pool_hbm,
    panels,
    edges,
    edge_gain,
    total,
    snaps,
    omega_z,
    omega_y,
    band_y,
    band_x,
    pool,
    spread_y,
    lines,
    chunks,
    sems,
):
    shots, cells_z = wave.shape[:2]
    last = cells_z - REACH
    step = cells_z // blocks
    pairs = [
        (band_y_hbm, band_y),
        (band_x_hbm, band_x),
        (omega_y_hbm, omega_y),
        (omega_z_hbm, omega_z),
        (pool_hbm, pool),
    ]
    few = len(pairs)
    order = list(range(1, blocks - 1)) + [0, blocks - 1]
    for block in order:
        span = pl.ds(block * step, step)
        pairs.append((snaps_hbm.at[:, :, span], snaps.at[:, :, span]))
    copies = fetch(pairs, sems)
    total[...] = jnp.zeros_like(total)
    for copy in copies[:few]:
        copy.wait()
    spread_y[...] = omega_y[...].astype(F32).astype(BF16)

    def gradients_at(z):
        laps = along_xy([wave[shot, z] for shot in range(shots)], band_y, band_x)
        gradients = []
        for shot in range(shots):
            lap = laps[shot] + along_z(wave, shot, z, cells_z)
            now = wave[shot, z]
            later = gain_self[z] * now + rest[shot, z] + gain_lap[z] * lap
            gradients.append(
                now * snaps[shot, 0, z].astype(F32) + later * snaps[shot, 1, z].astype(F32)
            )
        return gradients

    def middle_layer(z):
        weight_z = omega_z[pl.ds(z, 1), :].astype(F32)
        emit(gradients_at(z), z - REACH, spread_y, weight_z, pool, chunks, total, lines)

    def edge_layer(index):
        z = index + jnp.where(index >= REACH, last - REACH, 0)
        gradients = gradients_at(z)
        for shot in range(shots):
            edges[shot, index] = gradients[shot]
            edge_gain[shot, index] = gain_lap[z] * snaps[shot, 1, z].astype(F32)

    for place, block in enumerate(order[:-2]):
        copies[few + place].wait()
        pl.loop(block * step, (block + 1) * step)(middle_layer)
    send = pltpu.make_async_copy(
        chunks, panels.at[:, :, pl.ds(0, chunks.shape[2])], sems.at[len(pairs)]
    )
    send.start()
    for copy in copies[few + blocks - 2 :]:
        copy.wait()
    pl.loop(0, 2 * REACH)(edge_layer)
    send.wait()


def finish_kernel(
    panels_before,
    edges,
    edge_gain,
    near,
    far,
    omega_z,
    omega_y,
    pool,
    before,
    panels,
    total,
    spread_y,
    lines,
    chunks,
    sem,
):
    shots = edges.shape[0]
    cells_z = omega_z.shape[0]
    spread_y[...] = omega_y[...].astype(F32).astype(BF16)
    total[...] = before[...]
    is_odd = odd_slab() == 1
    part = chunks.shape[2]
    pieces = chunks.shape[0] // (2 * REACH)
    sends = []

    def halo(shot, upper):
        first, second = (far, near) if upper else (near, far)
        return lambda at: jnp.where(is_odd, first[shot, at], second[shot, at])

    for upper in (False, True):
        for layer in range(REACH):
            index = layer + (REACH if upper else 0)
            z = cells_z - REACH + layer if upper else layer
            gradients = [
                edges[shot, index]
                + edge_gain[shot, index] * halo_terms(halo(shot, upper), layer, upper)
                for shot in range(shots)
            ]
            weight_z = omega_z[z : z + 1, :].astype(F32)
            emit(gradients, index, spread_y, weight_z, pool, chunks, total, lines)
            span = pl.ds(index * pieces, pieces)
            send = pltpu.make_async_copy(
                chunks.at[span], panels.at[span, :, pl.ds(part, part)], sem.at[index]
            )
            send.start()
            sends.append(send)
    for send in sends:
        send.wait()


def sketch_kernel(total, omega_x, sketch):
    weights_x = omega_x[...].astype(F32)
    for shot in range(sketch.shape[0]):
        sketch[shot : shot + 1, :] = jnp.sum(total[shot] * weights_x, axis=0, keepdims=True)


def gram_kernel(panels, coarse, sketch, out):
    del coarse, sketch
    shots = out.shape[0]
    part = panels.shape[0] // shots
    width = 8
    gram = None
    for start in range(0, part, width):
        rows = [panels[pl.ds(start + index, shots, stride=part), :] for index in range(width)]
        high, low = two_parts(jnp.concatenate(rows, axis=1))
        both = jnp.concatenate([high, low], axis=0)
        term = dot_rows(both, both)
        gram = term if gram is None else gram + term
    folded = (gram[:shots, :shots] + gram[shots:, shots:]) + (
        gram[:shots, shots:] + gram[shots:, :shots]
    )
    out[...] = jnp.zeros_like(out)
    out[:, :shots] = folded


def gather_kernel(mine, sketch, out):
    shots = sketch.shape[0]
    total = mine[0]
    for source in range(1, mine.shape[0]):
        total = total + mine[source]
    for target in range(out.shape[0]):
        out[target, :shots] = sketch[...]
        out[target, shots:] = total


def output_kernel(
    groups, sketch_scale, gram_scale, terms, sketch_hbm, gram_hbm, sketch, gram_band, sems
):
    shots, _, lags = gram_band.shape
    lanes = terms.shape[2]
    total = terms[0]
    for source in range(1, terms.shape[0]):
        total = total + terms[source]
    sketch[...] = total[:shots] * sketch_scale
    group = lax.axis_index("shot")
    lag = lax.broadcasted_iota(jnp.int32, (lags, lanes), 0)
    lane = lax.broadcasted_iota(jnp.int32, (lags, lanes), 1)
    partner = group - 1 - lag
    partner = jnp.where(partner < 0, partner + groups, partner)
    for shot in range(shots):
        row = total[shots + shot : shots + shot + 1] * gram_scale
        for other in range(shots):
            wanted = lane == partner * shots + other
            picked = jnp.sum(jnp.where(wanted, row, 0.0), axis=1, keepdims=True)
            turned = jnp.sum(jnp.where(lane == lag, picked, 0.0), axis=0, keepdims=True)
            gram_band[shot, other : other + 1, :] = turned[:, :lags]
    for copy in fetch([(sketch, sketch_hbm), (gram_band, gram_hbm)], sems):
        copy.wait()


def spec(block=None, index=None):
    if block is None:
        return pl.BlockSpec(memory_space=pltpu.VMEM)
    return pl.BlockSpec(block, lambda step: index)


def run(kernel, out_shape, in_specs, out_specs, scratch=(), flops=0, moved=0, grid=None, **options):
    if grid is not None:
        options["grid"] = grid
    return pl.pallas_call(
        kernel,
        out_shape=out_shape,
        in_specs=in_specs,
        out_specs=out_specs,
        scratch_shapes=scratch,
        compiler_params=pltpu.CompilerParams(vmem_limit_bytes=VMEM_BYTES),
        cost_estimate=pl.CostEstimate(flops=flops, bytes_accessed=moved, transcendentals=0),
        **options,
    )


def local(
    courant,
    adj_prev,
    adj_curr,
    forward_snaps,
    traces,
    receiver_z,
    receiver_x,
    receiver_y,
    pml_cells,
    omega_z,
    omega_x,
    omega_y,
):
    shots, cells_z, cells_x, cells_y = adj_curr.shape
    slabs = lax.axis_size("slab")
    groups = lax.axis_size("shot")
    total_z = cells_z * slabs
    last = cells_z - REACH
    inner = last - REACH
    rank = omega_z.shape[1]
    receivers = traces.shape[2]
    half_x = cells_x // 2
    part = inner * half_x // groups
    blocks = cells_z // REACH
    shape = jax.ShapeDtypeStruct
    plane = (cells_x, cells_y)
    band = band_matrix(cells_y)
    band_y = jnp.asarray(np.concatenate([band, band], axis=0))
    band = band_matrix(cells_x)
    band_x = jnp.asarray(np.concatenate([band, band], axis=1))
    pool = jnp.asarray(pool_matrix(cells_y))

    def with_near(layers):
        return lax.ppermute(layers, "slab", [(i, i ^ 1) for i in range(slabs)])

    def with_far(layers):
        pairs = [(i, i + 1) for i in range(1, slabs - 1, 2)]
        return lax.ppermute(layers, "slab", pairs + [(j, i) for i, j in pairs])

    vmem = spec()
    hbm = pl.BlockSpec(memory_space=pltpu.HBM)

    def pinned(*arrays):
        return [pltpu.with_memory_space_constraint(array, pltpu.HBM) for array in arrays]

    field = shape((shots, cells_z) + plane, F32)
    gain = shape((cells_z,) + plane, F32)
    edge = shape((shots, REACH) + plane, F32)
    like = lambda array: pltpu.VMEM(array.shape, array.dtype)
    near, far = run(
        slice_kernel,
        [edge, edge],
        in_specs=[hbm],
        out_specs=[vmem, vmem],
        scratch=[pltpu.SemaphoreType.DMA((2,))],
        moved=2**21,
    )(*pinned(adj_curr))
    far = with_far(far)
    near = with_near(near)
    updated, rest, gain_self, gain_lap = run(
        functools.partial(begin_kernel, total_z, blocks),
        [field, field, gain, gain],
        in_specs=[pl.BlockSpec(memory_space=pltpu.SMEM)] + [hbm] * 9,
        out_specs=[vmem] * 4,
        scratch=[
            like(adj_curr),
            like(courant),
            like(adj_prev),
            like(traces),
            like(receiver_z),
            like(receiver_x),
            like(receiver_y),
            like(band_y),
            like(band_x),
            pltpu.VMEM((cells_z, cells_y), F32),
            pltpu.VMEM(plane, F32),
            pltpu.VMEM((shots, 2 * cells_y, 2 * receivers), BF16),
            pltpu.SemaphoreType.DMA((6 + 3 * blocks,)),
        ],
        flops=2 * 10**9,
        moved=11 * 2**20,
    )(
        pml_cells,
        *pinned(
            adj_curr,
            courant,
            adj_prev,
            traces,
            receiver_z,
            receiver_x,
            receiver_y,
            band_y,
            band_x,
        ),
    )

    layers4 = (shots, REACH) + plane
    gains4 = (REACH,) + plane

    whole4 = spec(layers4, (0, 0, 0, 0))
    wave4 = pl.BlockSpec(layers4, lambda step: (0, step * (blocks - 1), 0, 0))
    wave, near, far = run(
        edge_kernel,
        [field, edge, edge],
        in_specs=[
            wave4,
            whole4,
            whole4,
            pl.BlockSpec(gains4, lambda step: (step * (blocks - 1), 0, 0)),
        ],
        out_specs=[wave4, whole4, whole4],
        grid=(2,),
        flops=10**7,
        moved=2 * 2**20,
        input_output_aliases={0: 0},
    )(updated, near, far, gain_lap)
    far = with_far(far)
    near = with_near(near)

    panel = shape((groups, shots, 2 * part, cells_y), F32)
    spread = shape((shots, cells_x, rank), F32)
    scratch_emit = [
        pltpu.VMEM((cells_y, rank), BF16),
        pltpu.VMEM((shots,) + plane, F32),
        pltpu.VMEM((groups, shots, part, cells_y), F32),
    ]
    both = shape((shots, 2 * REACH) + plane, F32)
    panels, edges, edge_gain, total_mid = run(
        functools.partial(middle_kernel, blocks),
        [panel, both, both, spread],
        in_specs=[vmem] * 4 + [hbm] * 6,
        out_specs=[hbm, vmem, vmem, vmem],
        scratch=[
            like(forward_snaps),
            like(omega_z),
            like(omega_y),
            like(band_y),
            like(band_x),
            like(pool),
        ]
        + scratch_emit
        + [pltpu.SemaphoreType.DMA((6 + blocks,))],
        flops=2 * 10**9,
        moved=11 * 2**20,
    )(
        wave,
        rest,
        gain_self,
        gain_lap,
        *pinned(forward_snaps, omega_z, omega_y, band_y, band_x, pool),
    )

    panels, total = run(
        finish_kernel,
        [panel, spread],
        in_specs=[hbm] + [vmem] * 8,
        out_specs=[hbm, vmem],
        scratch=scratch_emit + [pltpu.SemaphoreType.DMA((2 * REACH,))],
        flops=5 * 10**8,
        moved=5 * 2**20,
        input_output_aliases={0: 0},
    )(
        panels,
        edges,
        edge_gain,
        near,
        far,
        omega_z,
        omega_y,
        pool,
        total_mid,
    )
    sketch_part = run(
        sketch_kernel,
        shape((shots, rank), F32),
        in_specs=[vmem, vmem],
        out_specs=vmem,
        flops=2 * 10**5,
        moved=2**18,
    )(total, omega_x)
    got = lax.all_to_all(panels, "shot", 0, 0, tiled=True)

    folded = panels.reshape(inner, half_x // part, shots, 2, part, cells_y)
    folded = folded.transpose(3, 2, 0, 1, 4, 5).reshape(2, shots, inner, half_x, cells_y)
    coarse = jnp.concatenate(
        [folded[1, :, :REACH], folded[0], folded[1, :, REACH:]], axis=1
    ).reshape(shots, cells_z, half_x * cells_y)

    all_shots = groups * shots
    gram = run(
        gram_kernel,
        shape((all_shots, cells_y), F32),
        in_specs=[vmem, hbm, hbm],
        out_specs=vmem,
        flops=10**8,
        moved=2**20,
    )(got.reshape(all_shots * 2 * part, cells_y), *pinned(coarse, sketch_part))
    mine = lax.all_to_all(gram.reshape(groups, shots, cells_y), "shot", 0, 0, tiled=True)
    terms = run(
        gather_kernel,
        shape((slabs, 2 * shots, rank), F32),
        in_specs=[vmem, vmem],
        out_specs=vmem,
        moved=2**16,
    )(mine, sketch_part)
    terms = lax.all_to_all(terms, "slab", 0, 0, tiled=True)
    sketch, gram_band = run(
        functools.partial(
            output_kernel,
            groups,
            1.0 / math.sqrt(total_z * cells_x * cells_y),
            1.0 / math.sqrt(total_z * cells_x * cells_y // 2),
        ),
        [shape((shots, rank), F32), shape((shots, shots, LAGS), F32)],
        in_specs=[vmem],
        out_specs=[hbm, hbm],
        scratch=[
            pltpu.VMEM((shots, rank), F32),
            pltpu.VMEM((shots, shots, LAGS), F32),
            pltpu.SemaphoreType.DMA((2,)),
        ],
        moved=2**16,
    )(terms)
    return (sketch, coarse, gram_band.transpose(0, 2, 1))


def solution(mesh):
    return jax.shard_map(
        local,
        mesh=mesh,
        in_specs=(
            P("slab", None, None),
            P("shot", "slab", None, None),
            P("shot", "slab", None, None),
            P("shot", None, "slab", None, None),
            P("shot", None, None),
            P("shot", None),
            P("shot", None),
            P("shot", None),
            P(),
            P("slab", None),
            P(),
            P(),
        ),
        out_specs=(P("shot", None), P("shot", "slab", None), P("shot", None, None)),
        check_vma=False,
    )
```

```python
import functools
import math

import jax
import jax.numpy as jnp
import ml_dtypes
import numpy as np
from jax import lax
from jax.experimental import pallas as pl
from jax.experimental.pallas import tpu as pltpu
from jax.sharding import PartitionSpec as P

LAGS = 4
REACH = 4
WHOLE_TAPS = (None, 8064.0, -1008.0, 128.0, -9.0)
DIVISOR = 5040.0
CENTRE = 3.0 * (-205.0 / 72.0)
DAMP_PEAK = 0.3
F32 = jnp.float32
BF16 = jnp.bfloat16
VMEM_BYTES = 24 * 1024 * 1024


def band_matrix(cells):
    index = np.arange(cells)
    apart = np.abs(index[:, None] - index[None, :])
    band = np.zeros((cells, cells), np.float32)
    for offset in range(1, REACH + 1):
        band[apart == offset] = WHOLE_TAPS[offset]
    return band.astype(ml_dtypes.bfloat16)


def pool_matrix(cells_y):
    half = cells_y // 2
    pool = np.zeros((2 * cells_y, 2 * half), np.float32)
    index = np.arange(cells_y)
    pool[index, index // 2] = 0.5
    pool[cells_y + index, half + index // 2] = 0.5
    return pool.astype(ml_dtypes.bfloat16)


def dot(left, right):
    return lax.dot_general(left, right, (((1,), (0,)), ((), ())), preferred_element_type=F32)


def dot_rows(left, right):
    return lax.dot_general(left, right, (((1,), (1,)), ((), ())), preferred_element_type=F32)


def two_parts(values):
    high = values.astype(BF16)
    low = (values - high.astype(F32)).astype(BF16)
    return high, low


def along_xy(planes, band_y, band_x):
    parts = [two_parts(plane) for plane in planes]
    rows = [jnp.concatenate(pair, axis=1) for pair in parts]
    columns = [jnp.concatenate(pair, axis=0) for pair in parts]
    over_y = dot(jnp.concatenate(rows, axis=0), band_y[...])
    over_x = dot(band_x[...], jnp.concatenate(columns, axis=1))
    cells_x, cells_y = planes[0].shape
    return [
        over_y[shot * cells_x : (shot + 1) * cells_x] + over_x[:, shot * cells_y : (shot + 1) * cells_y]
        for shot in range(len(planes))
    ]


def along_z(field, shot, z, cells_z):
    total = None
    for offset in range(1, REACH + 1):
        tap = WHOLE_TAPS[offset]
        below = jnp.where(z - offset >= 0, tap, 0.0)
        above = jnp.where(z + offset < cells_z, tap, 0.0)
        term = below * field[shot, jnp.maximum(z - offset, 0)]
        term += above * field[shot, jnp.minimum(z + offset, cells_z - 1)]
        total = term if total is None else total + term
    return total


def ramp_squared(index, length, thickness):
    distance = jnp.minimum(index, length - 1 - index).astype(F32)
    reach = jnp.full(index.shape, thickness, jnp.int32).astype(F32)
    ramp = jnp.maximum((reach - distance) / reach, 0.0)
    return ramp * ramp


def fetch(pairs, sems):
    copies = [
        pltpu.make_async_copy(source, target, sems.at[index])
        for index, (source, target) in enumerate(pairs)
    ]
    for copy in copies:
        copy.start()
    return copies


def begin_kernel(
    total_z,
    blocks,
    pml,
    curr_hbm,
    courant_hbm,
    prev_hbm,
    traces_hbm,
    place_z_hbm,
    place_x_hbm,
    place_y_hbm,
    band_y_hbm,
    band_x_hbm,
    updated,
    rest,
    gain_self,
    gain_lap,
    curr,
    courant,
    prev,
    traces,
    place_z,
    place_x,
    place_y,
    band_y,
    band_x,
    ramp_z,
    ramp_xy,
    inject,
    sems,
):
    cells_z, cells_x, cells_y = courant.shape
    shots = curr.shape[0]
    step = cells_z // blocks
    pairs = [
        (traces_hbm, traces),
        (place_z_hbm, place_z),
        (place_x_hbm, place_x),
        (place_y_hbm, place_y),
        (band_y_hbm, band_y),
        (band_x_hbm, band_x),
    ]
    few = len(pairs)
    for block in range(blocks):
        span = pl.ds(block * step, step)
        pairs.append((curr_hbm.at[:, span], curr.at[:, span]))
        pairs.append((courant_hbm.at[span], courant.at[span]))
        pairs.append((prev_hbm.at[:, span], prev.at[:, span]))
    copies = fetch(pairs, sems)
    first_z = lax.axis_index("slab") * cells_z
    plane = (cells_x, cells_y)
    row = lax.broadcasted_iota(jnp.int32, plane, 0)
    column = lax.broadcasted_iota(jnp.int32, plane, 1)
    ramp_z[...] = ramp_squared(
        lax.broadcasted_iota(jnp.int32, ramp_z.shape, 0) + first_z, total_z, pml[0]
    )
    ramp_xy[...] = ramp_squared(row, cells_x, pml[1]) + ramp_squared(column, cells_y, pml[2])
    for copy in copies[:few]:
        copy.wait()
    receivers = traces.shape[2]
    cell = lax.broadcasted_iota(jnp.int32, (cells_y, receivers), 0)
    for shot in range(shots):
        here = cell == place_y[shot : shot + 1, :]
        for instant in range(2):
            high, low = two_parts(jnp.where(here, traces[shot, instant : instant + 1, :], 0.0))
            span = slice(instant * cells_y, (instant + 1) * cells_y)
            inject[shot, span, :receivers] = high
            inject[shot, span, receivers:] = low
    line = lax.broadcasted_iota(jnp.int32, (cells_x, receivers), 0)

    def one_layer(z):
        damping = DAMP_PEAK * (ramp_z[pl.ds(z, 1), :] + ramp_xy[...])
        scale = 1.0 / (1.0 + damping)
        speed = courant[z]
        lap_gain = scale * (speed * speed)
        self_gain = 2.0 * scale + CENTRE * lap_gain
        lap_gain = lap_gain * (1.0 / DIVISOR)
        prev_gain = scale * (1.0 - damping)
        gain_self[z] = self_gain
        gain_lap[z] = lap_gain
        laps = along_xy([curr[shot, z] for shot in range(shots)], band_y, band_x)
        for shot in range(shots):
            now = curr[shot, z]
            lap = laps[shot] + along_z(curr, shot, z, cells_z)
            code = (place_z[shot : shot + 1, :] - first_z - z) * cells_x + place_x[shot : shot + 1, :]
            mark = jnp.where(line == code, 1.0, 0.0).astype(BF16)
            source = dot_rows(jnp.concatenate([mark, mark], axis=1), inject[shot])
            updated[shot, z] = (
                self_gain * now
                - prev_gain * prev[shot, z]
                + lap_gain * lap
                + scale * source[:, :cells_y]
            )
            rest[shot, z] = scale * source[:, cells_y:] - prev_gain * now

    copies[few].wait()
    for block in range(blocks):
        if block + 1 < blocks:
            copies[few + 3 * block + 3].wait()
        for copy in copies[few + 3 * block + 1 : few + 3 * block + 3]:
            copy.wait()
        pl.loop(block * step, (block + 1) * step)(one_layer)


def odd_slab():
    return lax.rem(lax.axis_index("slab"), 2)


def slice_kernel(curr, near, far, sems):
    layers = near.shape[1]
    last = curr.shape[1] - layers
    odd = odd_slab()
    copies = fetch(
        [
            (curr.at[:, pl.ds((1 - odd) * last, layers)], near),
            (curr.at[:, pl.ds(odd * last, layers)], far),
        ],
        sems,
    )
    for copy in copies:
        copy.wait()


def halo_terms(halo, layer, upper):
    total = None
    for offset in range(1, REACH + 1):
        at = layer + offset - REACH if upper else layer - offset + REACH
        if 0 <= at < REACH:
            term = WHOLE_TAPS[offset] * halo(at)
            total = term if total is None else total + term
    return total


def edge_kernel(partial, near, far, gain_lap, whole, near_out, far_out):
    odd = odd_slab()
    step = pl.program_id(0)
    for upper in (False, True):
        for halo, out, parity in (
            (near, near_out, 0 if upper else 1),
            (far, far_out, 1 if upper else 0),
        ):

            @pl.when((step == int(upper)) & (odd == parity))
            def _():
                @pl.loop(0, partial.shape[0])
                def _(shot):
                    for layer in range(REACH):
                        terms = halo_terms(lambda at: halo[shot, at], layer, upper)
                        value = partial[shot, layer] + gain_lap[layer] * terms
                        whole[shot, layer] = value
                        out[shot, layer] = value


def emit(gradients, layer, spread_y, weight_z, pool, chunks, total, lines):
    shots = len(gradients)
    rounded = [gradient.astype(BF16) for gradient in gradients]
    cells_x = rounded[0].shape[0]
    spread = dot(jnp.concatenate(rounded, axis=0), spread_y[...])
    half = cells_x // 2
    pairs = []
    for shot in range(shots):
        total[shot] += spread[shot * cells_x : (shot + 1) * cells_x] * weight_z
        lines[shot] = rounded[shot].astype(F32)
        even = lines[shot, pl.ds(0, half, stride=2), :].astype(BF16)
        odd = lines[shot, pl.ds(1, half, stride=2), :].astype(BF16)
        pairs.append(jnp.concatenate([even, odd], axis=1))
    coarse = dot(jnp.concatenate(pairs, axis=0), pool[...])
    part = chunks.shape[2]
    pieces = half // part
    for shot in range(shots):
        for piece in range(pieces):
            start = shot * half + piece * part
            chunks[layer * pieces + piece, shot] = coarse[start : start + part]


def middle_kernel(
    blocks,
    wave,
    rest,
    gain_self,
    gain_lap,
    snaps_hbm,
    omega_z_hbm,
    omega_y_hbm,
    band_y_hbm,
    band_x_hbm,
    pool_hbm,
    panels,
    edges,
    edge_gain,
    total,
    snaps,
    omega_z,
    omega_y,
    band_y,
    band_x,
    pool,
    spread_y,
    lines,
    chunks,
    sems,
):
    shots, cells_z = wave.shape[:2]
    last = cells_z - REACH
    step = cells_z // blocks
    pairs = [
        (band_y_hbm, band_y),
        (band_x_hbm, band_x),
        (omega_y_hbm, omega_y),
        (omega_z_hbm, omega_z),
        (pool_hbm, pool),
    ]
    few = len(pairs)
    order = list(range(1, blocks - 1)) + [0, blocks - 1]
    for block in order:
        span = pl.ds(block * step, step)
        pairs.append((snaps_hbm.at[:, :, span], snaps.at[:, :, span]))
    copies = fetch(pairs, sems)
    total[...] = jnp.zeros_like(total)
    for copy in copies[:few]:
        copy.wait()
    spread_y[...] = omega_y[...].astype(F32).astype(BF16)

    def gradients_at(z):
        laps = along_xy([wave[shot, z] for shot in range(shots)], band_y, band_x)
        gradients = []
        for shot in range(shots):
            lap = laps[shot] + along_z(wave, shot, z, cells_z)
            now = wave[shot, z]
            later = gain_self[z] * now + rest[shot, z] + gain_lap[z] * lap
            gradients.append(
                now * snaps[shot, 0, z].astype(F32) + later * snaps[shot, 1, z].astype(F32)
            )
        return gradients

    def middle_layer(z):
        weight_z = omega_z[pl.ds(z, 1), :].astype(F32)
        emit(gradients_at(z), z - REACH, spread_y, weight_z, pool, chunks, total, lines)

    def edge_layer(index):
        z = index + jnp.where(index >= REACH, last - REACH, 0)
        gradients = gradients_at(z)
        for shot in range(shots):
            edges[shot, index] = gradients[shot]
            edge_gain[shot, index] = gain_lap[z] * snaps[shot, 1, z].astype(F32)

    for place, block in enumerate(order[:-2]):
        copies[few + place].wait()
        pl.loop(block * step, (block + 1) * step)(middle_layer)
    send = pltpu.make_async_copy(
        chunks, panels.at[:, :, pl.ds(0, chunks.shape[2])], sems.at[len(pairs)]
    )
    send.start()
    for copy in copies[few + blocks - 2 :]:
        copy.wait()
    pl.loop(0, 2 * REACH)(edge_layer)
    send.wait()


def finish_kernel(
    is_far,
    panels_before,
    edges,
    edge_gain,
    halo,
    omega_z,
    omega_y,
    pool,
    before,
    panels,
    total,
    spread_y,
    lines,
    chunks,
    sem,
):
    shots = edges.shape[0]
    cells_z = omega_z.shape[0]
    spread_y[...] = omega_y[...].astype(F32).astype(BF16)
    total[...] = before[...]
    part = chunks.shape[2]
    pieces = chunks.shape[0] // (2 * REACH)
    for upper in (False, True):

        @pl.when(odd_slab() == int(upper == is_far))
        def _():
            sends = []
            for layer in range(REACH):
                index = layer + (REACH if upper else 0)
                z = cells_z - REACH + layer if upper else layer
                gradients = [
                    edges[shot, index]
                    + edge_gain[shot, index]
                    * halo_terms(lambda at: halo[shot, at], layer, upper)
                    for shot in range(shots)
                ]
                weight_z = omega_z[z : z + 1, :].astype(F32)
                emit(gradients, index, spread_y, weight_z, pool, chunks, total, lines)
                span = pl.ds(index * pieces, pieces)
                send = pltpu.make_async_copy(
                    chunks.at[span], panels.at[span, :, pl.ds(part, part)], sem.at[layer]
                )
                send.start()
                sends.append(send)
            for send in sends:
                send.wait()


def sketch_kernel(total, omega_x, sketch):
    weights_x = omega_x[...].astype(F32)
    for shot in range(sketch.shape[0]):
        sketch[shot : shot + 1, :] = jnp.sum(total[shot] * weights_x, axis=0, keepdims=True)


def gram_kernel(panels, coarse, sketch, out):
    del coarse, sketch
    shots = out.shape[0]
    part = panels.shape[0] // shots
    width = 8
    gram = None
    for start in range(0, part, width):
        rows = [panels[pl.ds(start + index, shots, stride=part), :] for index in range(width)]
        high, low = two_parts(jnp.concatenate(rows, axis=1))
        both = jnp.concatenate([high, low], axis=0)
        term = dot_rows(both, both)
        gram = term if gram is None else gram + term
    folded = (gram[:shots, :shots] + gram[shots:, shots:]) + (
        gram[:shots, shots:] + gram[shots:, :shots]
    )
    out[...] = jnp.zeros_like(out)
    out[:, :shots] = folded


def gather_kernel(mine, sketch, out):
    shots = sketch.shape[0]
    total = mine[0]
    for source in range(1, mine.shape[0]):
        total = total + mine[source]
    for target in range(out.shape[0]):
        out[target, :shots] = sketch[...]
        out[target, shots:] = total


def output_kernel(
    groups, sketch_scale, gram_scale, terms, sketch_hbm, gram_hbm, sketch, gram_band, sems
):
    shots, _, lags = gram_band.shape
    lanes = terms.shape[2]
    total = terms[0]
    for source in range(1, terms.shape[0]):
        total = total + terms[source]
    sketch[...] = total[:shots] * sketch_scale
    group = lax.axis_index("shot")
    lag = lax.broadcasted_iota(jnp.int32, (lags, lanes), 0)
    lane = lax.broadcasted_iota(jnp.int32, (lags, lanes), 1)
    partner = group - 1 - lag
    partner = jnp.where(partner < 0, partner + groups, partner)
    for shot in range(shots):
        row = total[shots + shot : shots + shot + 1] * gram_scale
        for other in range(shots):
            wanted = lane == partner * shots + other
            picked = jnp.sum(jnp.where(wanted, row, 0.0), axis=1, keepdims=True)
            turned = jnp.sum(jnp.where(lane == lag, picked, 0.0), axis=0, keepdims=True)
            gram_band[shot, other : other + 1, :] = turned[:, :lags]
    for copy in fetch([(sketch, sketch_hbm), (gram_band, gram_hbm)], sems):
        copy.wait()


def spec(block=None, index=None):
    if block is None:
        return pl.BlockSpec(memory_space=pltpu.VMEM)
    return pl.BlockSpec(block, lambda step: index)


def run(kernel, out_shape, in_specs, out_specs, scratch=(), flops=0, moved=0, grid=None, **options):
    if grid is not None:
        options["grid"] = grid
    return pl.pallas_call(
        kernel,
        out_shape=out_shape,
        in_specs=in_specs,
        out_specs=out_specs,
        scratch_shapes=scratch,
        compiler_params=pltpu.CompilerParams(vmem_limit_bytes=VMEM_BYTES),
        cost_estimate=pl.CostEstimate(flops=flops, bytes_accessed=moved, transcendentals=0),
        **options,
    )


def local(
    courant,
    adj_prev,
    adj_curr,
    forward_snaps,
    traces,
    receiver_z,
    receiver_x,
    receiver_y,
    pml_cells,
    omega_z,
    omega_x,
    omega_y,
):
    shots, cells_z, cells_x, cells_y = adj_curr.shape
    slabs = lax.axis_size("slab")
    groups = lax.axis_size("shot")
    total_z = cells_z * slabs
    last = cells_z - REACH
    inner = last - REACH
    rank = omega_z.shape[1]
    receivers = traces.shape[2]
    half_x = cells_x // 2
    part = inner * half_x // groups
    blocks = cells_z // REACH
    shape = jax.ShapeDtypeStruct
    plane = (cells_x, cells_y)
    band = band_matrix(cells_y)
    band_y = jnp.asarray(np.concatenate([band, band], axis=0))
    band = band_matrix(cells_x)
    band_x = jnp.asarray(np.concatenate([band, band], axis=1))
    pool = jnp.asarray(pool_matrix(cells_y))

    def with_near(layers):
        return lax.ppermute(layers, "slab", [(i, i ^ 1) for i in range(slabs)])

    def with_far(layers):
        pairs = [(i, i + 1) for i in range(1, slabs - 1, 2)]
        return lax.ppermute(layers, "slab", pairs + [(j, i) for i, j in pairs])

    vmem = spec()
    hbm = pl.BlockSpec(memory_space=pltpu.HBM)

    def pinned(*arrays):
        return [pltpu.with_memory_space_constraint(array, pltpu.HBM) for array in arrays]

    field = shape((shots, cells_z) + plane, F32)
    gain = shape((cells_z,) + plane, F32)
    edge = shape((shots, REACH) + plane, F32)
    like = lambda array: pltpu.VMEM(array.shape, array.dtype)
    near, far = run(
        slice_kernel,
        [edge, edge],
        in_specs=[hbm],
        out_specs=[vmem, vmem],
        scratch=[pltpu.SemaphoreType.DMA((2,))],
        moved=2**21,
    )(*pinned(adj_curr))
    far = with_far(far)
    near = with_near(near)
    updated, rest, gain_self, gain_lap = run(
        functools.partial(begin_kernel, total_z, blocks),
        [field, field, gain, gain],
        in_specs=[pl.BlockSpec(memory_space=pltpu.SMEM)] + [hbm] * 9,
        out_specs=[vmem] * 4,
        scratch=[
            like(adj_curr),
            like(courant),
            like(adj_prev),
            like(traces),
            like(receiver_z),
            like(receiver_x),
            like(receiver_y),
            like(band_y),
            like(band_x),
            pltpu.VMEM((cells_z, cells_y), F32),
            pltpu.VMEM(plane, F32),
            pltpu.VMEM((shots, 2 * cells_y, 2 * receivers), BF16),
            pltpu.SemaphoreType.DMA((6 + 3 * blocks,)),
        ],
        flops=2 * 10**9,
        moved=11 * 2**20,
    )(
        pml_cells,
        *pinned(
            adj_curr,
            courant,
            adj_prev,
            traces,
            receiver_z,
            receiver_x,
            receiver_y,
            band_y,
            band_x,
        ),
    )

    layers4 = (shots, REACH) + plane
    gains4 = (REACH,) + plane

    whole4 = spec(layers4, (0, 0, 0, 0))
    wave4 = pl.BlockSpec(layers4, lambda step: (0, step * (blocks - 1), 0, 0))
    wave, near, far = run(
        edge_kernel,
        [field, edge, edge],
        in_specs=[
            wave4,
            whole4,
            whole4,
            pl.BlockSpec(gains4, lambda step: (step * (blocks - 1), 0, 0)),
        ],
        out_specs=[wave4, whole4, whole4],
        grid=(2,),
        flops=10**7,
        moved=2 * 2**20,
        input_output_aliases={0: 0},
    )(updated, near, far, gain_lap)
    far = with_far(far)
    near = with_near(near)

    panel = shape((groups, shots, 2 * part, cells_y), F32)
    spread = shape((shots, cells_x, rank), F32)
    scratch_emit = [
        pltpu.VMEM((cells_y, rank), BF16),
        pltpu.VMEM((shots,) + plane, F32),
        pltpu.VMEM((groups, shots, part, cells_y), F32),
    ]
    both = shape((shots, 2 * REACH) + plane, F32)
    panels, edges, edge_gain, total_mid = run(
        functools.partial(middle_kernel, blocks),
        [panel, both, both, spread],
        in_specs=[vmem] * 4 + [hbm] * 6,
        out_specs=[hbm, vmem, vmem, vmem],
        scratch=[
            like(forward_snaps),
            like(omega_z),
            like(omega_y),
            like(band_y),
            like(band_x),
            like(pool),
        ]
        + scratch_emit
        + [pltpu.SemaphoreType.DMA((6 + blocks,))],
        flops=2 * 10**9,
        moved=11 * 2**20,
    )(
        wave,
        rest,
        gain_self,
        gain_lap,
        *pinned(forward_snaps, omega_z, omega_y, band_y, band_x, pool),
    )

    def finish(is_far, panels, halo, total):
        return run(
            functools.partial(finish_kernel, is_far),
            [panel, spread],
            in_specs=[hbm] + [vmem] * 7,
            out_specs=[hbm, vmem],
            scratch=scratch_emit + [pltpu.SemaphoreType.DMA((REACH,))],
            flops=3 * 10**8,
            moved=3 * 2**20,
            input_output_aliases={0: 0},
        )(panels, edges, edge_gain, halo, omega_z, omega_y, pool, total)

    panels, total = finish(False, panels, near, total_mid)
    panels, total = finish(True, panels, far, total)
    sketch_part = run(
        sketch_kernel,
        shape((shots, rank), F32),
        in_specs=[vmem, vmem],
        out_specs=vmem,
        flops=2 * 10**5,
        moved=2**18,
    )(total, omega_x)
    got = lax.all_to_all(panels, "shot", 0, 0, tiled=True)

    folded = panels.reshape(inner, half_x // part, shots, 2, part, cells_y)
    folded = folded.transpose(3, 2, 0, 1, 4, 5).reshape(2, shots, inner, half_x, cells_y)
    coarse = jnp.concatenate(
        [folded[1, :, :REACH], folded[0], folded[1, :, REACH:]], axis=1
    ).reshape(shots, cells_z, half_x * cells_y)

    all_shots = groups * shots
    gram = run(
        gram_kernel,
        shape((all_shots, cells_y), F32),
        in_specs=[vmem, hbm, hbm],
        out_specs=vmem,
        flops=10**8,
        moved=2**20,
    )(got.reshape(all_shots * 2 * part, cells_y), *pinned(coarse, sketch_part))
    mine = lax.all_to_all(gram.reshape(groups, shots, cells_y), "shot", 0, 0, tiled=True)
    terms = run(
        gather_kernel,
        shape((slabs, 2 * shots, rank), F32),
        in_specs=[vmem, vmem],
        out_specs=vmem,
        moved=2**16,
    )(mine, sketch_part)
    terms = lax.all_to_all(terms, "slab", 0, 0, tiled=True)
    sketch, gram_band = run(
        functools.partial(
            output_kernel,
            groups,
            1.0 / math.sqrt(total_z * cells_x * cells_y),
            1.0 / math.sqrt(total_z * cells_x * cells_y // 2),
        ),
        [shape((shots, rank), F32), shape((shots, shots, LAGS), F32)],
        in_specs=[vmem],
        out_specs=[hbm, hbm],
        scratch=[
            pltpu.VMEM((shots, rank), F32),
            pltpu.VMEM((shots, shots, LAGS), F32),
            pltpu.SemaphoreType.DMA((2,)),
        ],
        moved=2**16,
    )(terms)
    return (sketch, coarse, gram_band.transpose(0, 2, 1))


def solution(mesh):
    return jax.shard_map(
        local,
        mesh=mesh,
        in_specs=(
            P("slab", None, None),
            P("shot", "slab", None, None),
            P("shot", "slab", None, None),
            P("shot", None, "slab", None, None),
            P("shot", None, None),
            P("shot", None),
            P("shot", None),
            P("shot", None),
            P(),
            P("slab", None),
            P(),
            P(),
        ),
        out_specs=(P("shot", None), P("shot", "slab", None), P("shot", None, None)),
        check_vma=False,
    )
```

```python
import functools
import math

import jax
import jax.numpy as jnp
import ml_dtypes
import numpy as np
from jax import lax
from jax.experimental import pallas as pl
from jax.experimental.pallas import tpu as pltpu
from jax.sharding import PartitionSpec as P

LAGS = 4
REACH = 4
WHOLE_TAPS = (None, 8064.0, -1008.0, 128.0, -9.0)
DIVISOR = 5040.0
CENTRE = 3.0 * (-205.0 / 72.0)
DAMP_PEAK = 0.3
F32 = jnp.float32
BF16 = jnp.bfloat16
VMEM_BYTES = 24 * 1024 * 1024


def band_matrix(cells):
    index = np.arange(cells)
    apart = np.abs(index[:, None] - index[None, :])
    band = np.zeros((cells, cells), np.float32)
    for offset in range(1, REACH + 1):
        band[apart == offset] = WHOLE_TAPS[offset]
    return band.astype(ml_dtypes.bfloat16)


def pool_matrix(cells_y):
    half = cells_y // 2
    pool = np.zeros((2 * cells_y, 2 * half), np.float32)
    index = np.arange(cells_y)
    pool[index, index // 2] = 0.5
    pool[cells_y + index, half + index // 2] = 0.5
    return pool.astype(ml_dtypes.bfloat16)


def dot(left, right):
    return lax.dot_general(left, right, (((1,), (0,)), ((), ())), preferred_element_type=F32)


def dot_rows(left, right):
    return lax.dot_general(left, right, (((1,), (1,)), ((), ())), preferred_element_type=F32)


def two_parts(values):
    high = values.astype(BF16)
    low = (values - high.astype(F32)).astype(BF16)
    return high, low


def along_xy(planes, band_y, band_x):
    parts = [two_parts(plane) for plane in planes]
    rows = [jnp.concatenate(pair, axis=1) for pair in parts]
    columns = [jnp.concatenate(pair, axis=0) for pair in parts]
    over_y = dot(jnp.concatenate(rows, axis=0), band_y[...])
    over_x = dot(band_x[...], jnp.concatenate(columns, axis=1))
    cells_x, cells_y = planes[0].shape
    return [
        over_y[shot * cells_x : (shot + 1) * cells_x] + over_x[:, shot * cells_y : (shot + 1) * cells_y]
        for shot in range(len(planes))
    ]


def along_z(field, shot, z, cells_z):
    total = None
    for offset in range(1, REACH + 1):
        tap = WHOLE_TAPS[offset]
        below = jnp.where(z - offset >= 0, tap, 0.0)
        above = jnp.where(z + offset < cells_z, tap, 0.0)
        term = below * field[shot, jnp.maximum(z - offset, 0)]
        term += above * field[shot, jnp.minimum(z + offset, cells_z - 1)]
        total = term if total is None else total + term
    return total


def ramp_squared(index, length, thickness):
    distance = jnp.minimum(index, length - 1 - index).astype(F32)
    reach = jnp.full(index.shape, thickness, jnp.int32).astype(F32)
    ramp = jnp.maximum((reach - distance) / reach, 0.0)
    return ramp * ramp


def fetch(pairs, sems):
    copies = [
        pltpu.make_async_copy(source, target, sems.at[index])
        for index, (source, target) in enumerate(pairs)
    ]
    for copy in copies:
        copy.start()
    return copies


def begin_kernel(
    total_z,
    blocks,
    pml,
    curr_hbm,
    courant_hbm,
    prev_hbm,
    traces_hbm,
    place_z_hbm,
    place_x_hbm,
    place_y_hbm,
    band_y_hbm,
    band_x_hbm,
    updated,
    rest,
    gain_self,
    gain_lap,
    curr,
    courant,
    prev,
    traces,
    place_z,
    place_x,
    place_y,
    band_y,
    band_x,
    ramp_z,
    ramp_xy,
    inject,
    sems,
):
    cells_z, cells_x, cells_y = courant.shape
    shots = curr.shape[0]
    step = cells_z // blocks
    pairs = [
        (traces_hbm, traces),
        (place_z_hbm, place_z),
        (place_x_hbm, place_x),
        (place_y_hbm, place_y),
        (band_y_hbm, band_y),
        (band_x_hbm, band_x),
    ]
    few = len(pairs)
    for block in range(blocks):
        span = pl.ds(block * step, step)
        pairs.append((curr_hbm.at[:, span], curr.at[:, span]))
        pairs.append((courant_hbm.at[span], courant.at[span]))
        pairs.append((prev_hbm.at[:, span], prev.at[:, span]))
    copies = fetch(pairs, sems)
    first_z = lax.axis_index("slab") * cells_z
    plane = (cells_x, cells_y)
    row = lax.broadcasted_iota(jnp.int32, plane, 0)
    column = lax.broadcasted_iota(jnp.int32, plane, 1)
    ramp_z[...] = ramp_squared(
        lax.broadcasted_iota(jnp.int32, ramp_z.shape, 0) + first_z, total_z, pml[0]
    )
    ramp_xy[...] = ramp_squared(row, cells_x, pml[1]) + ramp_squared(column, cells_y, pml[2])
    for copy in copies[:few]:
        copy.wait()
    receivers = traces.shape[2]
    cell = lax.broadcasted_iota(jnp.int32, (cells_y, receivers), 0)
    for shot in range(shots):
        here = cell == place_y[shot : shot + 1, :]
        for instant in range(2):
            high, low = two_parts(jnp.where(here, traces[shot, instant : instant + 1, :], 0.0))
            span = slice(instant * cells_y, (instant + 1) * cells_y)
            inject[shot, span, :receivers] = high
            inject[shot, span, receivers:] = low
    line = lax.broadcasted_iota(jnp.int32, (cells_x, receivers), 0)

    def one_layer(z):
        damping = DAMP_PEAK * (ramp_z[pl.ds(z, 1), :] + ramp_xy[...])
        scale = 1.0 / (1.0 + damping)
        speed = courant[z]
        lap_gain = scale * (speed * speed)
        self_gain = 2.0 * scale + CENTRE * lap_gain
        lap_gain = lap_gain * (1.0 / DIVISOR)
        prev_gain = scale * (1.0 - damping)
        gain_self[z] = self_gain
        gain_lap[z] = lap_gain
        laps = along_xy([curr[shot, z] for shot in range(shots)], band_y, band_x)
        for shot in range(shots):
            now = curr[shot, z]
            lap = laps[shot] + along_z(curr, shot, z, cells_z)
            code = (place_z[shot : shot + 1, :] - first_z - z) * cells_x + place_x[shot : shot + 1, :]
            mark = jnp.where(line == code, 1.0, 0.0).astype(BF16)
            source = dot_rows(jnp.concatenate([mark, mark], axis=1), inject[shot])
            updated[shot, z] = (
                self_gain * now
                - prev_gain * prev[shot, z]
                + lap_gain * lap
                + scale * source[:, :cells_y]
            )
            rest[shot, z] = scale * source[:, cells_y:] - prev_gain * now

    copies[few].wait()
    for block in range(blocks):
        if block + 1 < blocks:
            copies[few + 3 * block + 3].wait()
        for copy in copies[few + 3 * block + 1 : few + 3 * block + 3]:
            copy.wait()
        pl.loop(block * step, (block + 1) * step)(one_layer)


def odd_slab():
    return lax.rem(lax.axis_index("slab"), 2)


def slice_kernel(curr, near, far, sems):
    layers = near.shape[1]
    last = curr.shape[1] - layers
    odd = odd_slab()
    copies = fetch(
        [
            (curr.at[:, pl.ds((1 - odd) * last, layers)], near),
            (curr.at[:, pl.ds(odd * last, layers)], far),
        ],
        sems,
    )
    for copy in copies:
        copy.wait()


def halo_terms(halo, layer, upper):
    total = None
    for offset in range(1, REACH + 1):
        at = layer + offset - REACH if upper else layer - offset + REACH
        if 0 <= at < REACH:
            term = WHOLE_TAPS[offset] * halo(at)
            total = term if total is None else total + term
    return total


def edge_kernel(side, partial, halo, gain_lap, whole, out):
    for upper in (False, True):

        @pl.when(side[0] == int(upper))
        def _():
            @pl.loop(0, partial.shape[0])
            def _(shot):
                for layer in range(REACH):
                    terms = halo_terms(lambda at: halo[shot, at], layer, upper)
                    value = partial[shot, layer] + gain_lap[layer] * terms
                    whole[shot, layer] = value
                    out[shot, layer] = value


def emit(gradients, layer, spread_y, weight_z, pool, chunks, total, lines):
    shots = len(gradients)
    rounded = [gradient.astype(BF16) for gradient in gradients]
    cells_x = rounded[0].shape[0]
    spread = dot(jnp.concatenate(rounded, axis=0), spread_y[...])
    half = cells_x // 2
    pairs = []
    for shot in range(shots):
        total[shot] += spread[shot * cells_x : (shot + 1) * cells_x] * weight_z
        lines[shot] = rounded[shot].astype(F32)
        even = lines[shot, pl.ds(0, half, stride=2), :].astype(BF16)
        odd = lines[shot, pl.ds(1, half, stride=2), :].astype(BF16)
        pairs.append(jnp.concatenate([even, odd], axis=1))
    coarse = dot(jnp.concatenate(pairs, axis=0), pool[...])
    part = chunks.shape[2]
    pieces = half // part
    for shot in range(shots):
        for piece in range(pieces):
            start = shot * half + piece * part
            chunks[layer * pieces + piece, shot] = coarse[start : start + part]


def middle_kernel(
    blocks,
    wave,
    rest,
    gain_self,
    gain_lap,
    snaps_hbm,
    omega_z_hbm,
    omega_y_hbm,
    band_y_hbm,
    band_x_hbm,
    pool_hbm,
    panels,
    edges,
    edge_gain,
    total,
    snaps,
    omega_z,
    omega_y,
    band_y,
    band_x,
    pool,
    spread_y,
    lines,
    chunks,
    sems,
):
    shots, cells_z = wave.shape[:2]
    last = cells_z - REACH
    step = cells_z // blocks
    pairs = [
        (band_y_hbm, band_y),
        (band_x_hbm, band_x),
        (omega_y_hbm, omega_y),
        (omega_z_hbm, omega_z),
        (pool_hbm, pool),
    ]
    few = len(pairs)
    order = list(range(1, blocks - 1)) + [0, blocks - 1]
    for block in order:
        span = pl.ds(block * step, step)
        pairs.append((snaps_hbm.at[:, :, span], snaps.at[:, :, span]))
    copies = fetch(pairs, sems)
    total[...] = jnp.zeros_like(total)
    for copy in copies[:few]:
        copy.wait()
    spread_y[...] = omega_y[...].astype(F32).astype(BF16)

    def gradients_at(z):
        laps = along_xy([wave[shot, z] for shot in range(shots)], band_y, band_x)
        gradients = []
        for shot in range(shots):
            lap = laps[shot] + along_z(wave, shot, z, cells_z)
            now = wave[shot, z]
            later = gain_self[z] * now + rest[shot, z] + gain_lap[z] * lap
            gradients.append(
                now * snaps[shot, 0, z].astype(F32) + later * snaps[shot, 1, z].astype(F32)
            )
        return gradients

    def middle_layer(z):
        weight_z = omega_z[pl.ds(z, 1), :].astype(F32)
        emit(gradients_at(z), z - REACH, spread_y, weight_z, pool, chunks, total, lines)

    def edge_layer(index):
        z = index + jnp.where(index >= REACH, last - REACH, 0)
        gradients = gradients_at(z)
        for shot in range(shots):
            edges[shot, index] = gradients[shot]
            edge_gain[shot, index] = gain_lap[z] * snaps[shot, 1, z].astype(F32)

    for place, block in enumerate(order[:-2]):
        copies[few + place].wait()
        pl.loop(block * step, (block + 1) * step)(middle_layer)
    send = pltpu.make_async_copy(
        chunks, panels.at[:, :, pl.ds(0, chunks.shape[2])], sems.at[len(pairs)]
    )
    send.start()
    for copy in copies[few + blocks - 2 :]:
        copy.wait()
    pl.loop(0, 2 * REACH)(edge_layer)
    send.wait()


def finish_kernel(
    is_far,
    panels_before,
    edges,
    edge_gain,
    halo,
    omega_z,
    omega_y,
    pool,
    before,
    panels,
    total,
    spread_y,
    lines,
    chunks,
    sem,
):
    shots = edges.shape[0]
    cells_z = omega_z.shape[0]
    spread_y[...] = omega_y[...].astype(F32).astype(BF16)
    total[...] = before[...]
    part = chunks.shape[2]
    pieces = chunks.shape[0] // (2 * REACH)
    for upper in (False, True):

        @pl.when(odd_slab() == int(upper == is_far))
        def _():
            sends = []
            for layer in range(REACH):
                index = layer + (REACH if upper else 0)
                z = cells_z - REACH + layer if upper else layer
                gradients = [
                    edges[shot, index]
                    + edge_gain[shot, index]
                    * halo_terms(lambda at: halo[shot, at], layer, upper)
                    for shot in range(shots)
                ]
                weight_z = omega_z[z : z + 1, :].astype(F32)
                emit(gradients, index, spread_y, weight_z, pool, chunks, total, lines)
                span = pl.ds(index * pieces, pieces)
                send = pltpu.make_async_copy(
                    chunks.at[span], panels.at[span, :, pl.ds(part, part)], sem.at[layer]
                )
                send.start()
                sends.append(send)
            for send in sends:
                send.wait()


def sketch_kernel(total, omega_x, sketch):
    weights_x = omega_x[...].astype(F32)
    for shot in range(sketch.shape[0]):
        sketch[shot : shot + 1, :] = jnp.sum(total[shot] * weights_x, axis=0, keepdims=True)


def gram_kernel(panels, coarse, sketch, out):
    del coarse, sketch
    shots = out.shape[0]
    part = panels.shape[0] // shots
    width = 8
    gram = None
    for start in range(0, part, width):
        rows = [panels[pl.ds(start + index, shots, stride=part), :] for index in range(width)]
        high, low = two_parts(jnp.concatenate(rows, axis=1))
        both = jnp.concatenate([high, low], axis=0)
        term = dot_rows(both, both)
        gram = term if gram is None else gram + term
    folded = (gram[:shots, :shots] + gram[shots:, shots:]) + (
        gram[:shots, shots:] + gram[shots:, :shots]
    )
    out[...] = jnp.zeros_like(out)
    out[:, :shots] = folded


def gather_kernel(mine, sketch, out):
    shots = sketch.shape[0]
    total = mine[0]
    for source in range(1, mine.shape[0]):
        total = total + mine[source]
    for target in range(out.shape[0]):
        out[target, :shots] = sketch[...]
        out[target, shots:] = total


def output_kernel(
    groups, sketch_scale, gram_scale, terms, sketch_hbm, gram_hbm, sketch, gram_band, sems
):
    shots, _, lags = gram_band.shape
    lanes = terms.shape[2]
    total = terms[0]
    for source in range(1, terms.shape[0]):
        total = total + terms[source]
    sketch[...] = total[:shots] * sketch_scale
    group = lax.axis_index("shot")
    lag = lax.broadcasted_iota(jnp.int32, (lags, lanes), 0)
    lane = lax.broadcasted_iota(jnp.int32, (lags, lanes), 1)
    partner = group - 1 - lag
    partner = jnp.where(partner < 0, partner + groups, partner)
    for shot in range(shots):
        row = total[shots + shot : shots + shot + 1] * gram_scale
        for other in range(shots):
            wanted = lane == partner * shots + other
            picked = jnp.sum(jnp.where(wanted, row, 0.0), axis=1, keepdims=True)
            turned = jnp.sum(jnp.where(lane == lag, picked, 0.0), axis=0, keepdims=True)
            gram_band[shot, other : other + 1, :] = turned[:, :lags]
    for copy in fetch([(sketch, sketch_hbm), (gram_band, gram_hbm)], sems):
        copy.wait()


def spec(block=None, index=None):
    if block is None:
        return pl.BlockSpec(memory_space=pltpu.VMEM)
    return pl.BlockSpec(block, lambda step: index)


def run(kernel, out_shape, in_specs, out_specs, scratch=(), flops=0, moved=0, grid=None, **options):
    if grid is not None:
        options["grid"] = grid
    return pl.pallas_call(
        kernel,
        out_shape=out_shape,
        in_specs=in_specs,
        out_specs=out_specs,
        scratch_shapes=scratch,
        compiler_params=pltpu.CompilerParams(vmem_limit_bytes=VMEM_BYTES),
        cost_estimate=pl.CostEstimate(flops=flops, bytes_accessed=moved, transcendentals=0),
        **options,
    )


def local(
    courant,
    adj_prev,
    adj_curr,
    forward_snaps,
    traces,
    receiver_z,
    receiver_x,
    receiver_y,
    pml_cells,
    omega_z,
    omega_x,
    omega_y,
):
    shots, cells_z, cells_x, cells_y = adj_curr.shape
    slabs = lax.axis_size("slab")
    groups = lax.axis_size("shot")
    total_z = cells_z * slabs
    last = cells_z - REACH
    inner = last - REACH
    rank = omega_z.shape[1]
    receivers = traces.shape[2]
    half_x = cells_x // 2
    part = inner * half_x // groups
    blocks = cells_z // REACH
    shape = jax.ShapeDtypeStruct
    plane = (cells_x, cells_y)
    band = band_matrix(cells_y)
    band_y = jnp.asarray(np.concatenate([band, band], axis=0))
    band = band_matrix(cells_x)
    band_x = jnp.asarray(np.concatenate([band, band], axis=1))
    pool = jnp.asarray(pool_matrix(cells_y))

    def with_near(layers):
        return lax.ppermute(layers, "slab", [(i, i ^ 1) for i in range(slabs)])

    def with_far(layers):
        pairs = [(i, i + 1) for i in range(1, slabs - 1, 2)]
        return lax.ppermute(layers, "slab", pairs + [(j, i) for i, j in pairs])

    vmem = spec()
    hbm = pl.BlockSpec(memory_space=pltpu.HBM)

    def pinned(*arrays):
        return [pltpu.with_memory_space_constraint(array, pltpu.HBM) for array in arrays]

    field = shape((shots, cells_z) + plane, F32)
    gain = shape((cells_z,) + plane, F32)
    edge = shape((shots, REACH) + plane, F32)
    like = lambda array: pltpu.VMEM(array.shape, array.dtype)
    near, far = run(
        slice_kernel,
        [edge, edge],
        in_specs=[hbm],
        out_specs=[vmem, vmem],
        scratch=[pltpu.SemaphoreType.DMA((2,))],
        moved=2**21,
    )(*pinned(adj_curr))
    far = with_far(far)
    near = with_near(near)
    updated, rest, gain_self, gain_lap = run(
        functools.partial(begin_kernel, total_z, blocks),
        [field, field, gain, gain],
        in_specs=[pl.BlockSpec(memory_space=pltpu.SMEM)] + [hbm] * 9,
        out_specs=[vmem] * 4,
        scratch=[
            like(adj_curr),
            like(courant),
            like(adj_prev),
            like(traces),
            like(receiver_z),
            like(receiver_x),
            like(receiver_y),
            like(band_y),
            like(band_x),
            pltpu.VMEM((cells_z, cells_y), F32),
            pltpu.VMEM(plane, F32),
            pltpu.VMEM((shots, 2 * cells_y, 2 * receivers), BF16),
            pltpu.SemaphoreType.DMA((6 + 3 * blocks,)),
        ],
        flops=2 * 10**9,
        moved=11 * 2**20,
    )(
        pml_cells,
        *pinned(
            adj_curr,
            courant,
            adj_prev,
            traces,
            receiver_z,
            receiver_x,
            receiver_y,
            band_y,
            band_x,
        ),
    )

    layers4 = (shots, REACH) + plane
    gains4 = (REACH,) + plane

    whole4 = pl.BlockSpec(layers4, lambda step, side: (0, 0, 0, 0))
    wave4 = pl.BlockSpec(layers4, lambda step, side: (0, side[0] * (blocks - 1), 0, 0))

    def complete(side, wave, halo):
        return pl.pallas_call(
            edge_kernel,
            out_shape=[field, edge],
            grid_spec=pltpu.PrefetchScalarGridSpec(
                num_scalar_prefetch=1,
                grid=(1,),
                in_specs=[
                    wave4,
                    whole4,
                    pl.BlockSpec(gains4, lambda step, side: (side[0] * (blocks - 1), 0, 0)),
                ],
                out_specs=[wave4, whole4],
            ),
            compiler_params=pltpu.CompilerParams(vmem_limit_bytes=VMEM_BYTES),
            cost_estimate=pl.CostEstimate(
                flops=10**7, bytes_accessed=2 * 2**20, transcendentals=0
            ),
            input_output_aliases={1: 0},
        )(side, wave, halo, gain_lap)

    side = jnp.remainder(lax.axis_index("slab"), 2).astype(jnp.int32).reshape(1)
    wave, near = complete(1 - side, updated, near)
    wave, far = complete(side, wave, far)
    far = with_far(far)
    near = with_near(near)

    panel = shape((groups, shots, 2 * part, cells_y), F32)
    spread = shape((shots, cells_x, rank), F32)
    scratch_emit = [
        pltpu.VMEM((cells_y, rank), BF16),
        pltpu.VMEM((shots,) + plane, F32),
        pltpu.VMEM((groups, shots, part, cells_y), F32),
    ]
    both = shape((shots, 2 * REACH) + plane, F32)
    panels, edges, edge_gain, total_mid = run(
        functools.partial(middle_kernel, blocks),
        [panel, both, both, spread],
        in_specs=[vmem] * 4 + [hbm] * 6,
        out_specs=[hbm, vmem, vmem, vmem],
        scratch=[
            like(forward_snaps),
            like(omega_z),
            like(omega_y),
            like(band_y),
            like(band_x),
            like(pool),
        ]
        + scratch_emit
        + [pltpu.SemaphoreType.DMA((6 + blocks,))],
        flops=2 * 10**9,
        moved=11 * 2**20,
    )(
        wave,
        rest,
        gain_self,
        gain_lap,
        *pinned(forward_snaps, omega_z, omega_y, band_y, band_x, pool),
    )

    def finish(is_far, panels, halo, total):
        return run(
            functools.partial(finish_kernel, is_far),
            [panel, spread],
            in_specs=[hbm] + [vmem] * 7,
            out_specs=[hbm, vmem],
            scratch=scratch_emit + [pltpu.SemaphoreType.DMA((REACH,))],
            flops=3 * 10**8,
            moved=3 * 2**20,
            input_output_aliases={0: 0},
        )(panels, edges, edge_gain, halo, omega_z, omega_y, pool, total)

    panels, total = finish(False, panels, near, total_mid)
    panels, total = finish(True, panels, far, total)
    sketch_part = run(
        sketch_kernel,
        shape((shots, rank), F32),
        in_specs=[vmem, vmem],
        out_specs=vmem,
        flops=2 * 10**5,
        moved=2**18,
    )(total, omega_x)
    got = lax.all_to_all(panels, "shot", 0, 0, tiled=True)

    folded = panels.reshape(inner, half_x // part, shots, 2, part, cells_y)
    folded = folded.transpose(3, 2, 0, 1, 4, 5).reshape(2, shots, inner, half_x, cells_y)
    coarse = jnp.concatenate(
        [folded[1, :, :REACH], folded[0], folded[1, :, REACH:]], axis=1
    ).reshape(shots, cells_z, half_x * cells_y)

    all_shots = groups * shots
    gram = run(
        gram_kernel,
        shape((all_shots, cells_y), F32),
        in_specs=[vmem, hbm, hbm],
        out_specs=vmem,
        flops=10**8,
        moved=2**20,
    )(got.reshape(all_shots * 2 * part, cells_y), *pinned(coarse, sketch_part))
    mine = lax.all_to_all(gram.reshape(groups, shots, cells_y), "shot", 0, 0, tiled=True)
    terms = run(
        gather_kernel,
        shape((slabs, 2 * shots, rank), F32),
        in_specs=[vmem, vmem],
        out_specs=vmem,
        moved=2**16,
    )(mine, sketch_part)
    terms = lax.all_to_all(terms, "slab", 0, 0, tiled=True)
    sketch, gram_band = run(
        functools.partial(
            output_kernel,
            groups,
            1.0 / math.sqrt(total_z * cells_x * cells_y),
            1.0 / math.sqrt(total_z * cells_x * cells_y // 2),
        ),
        [shape((shots, rank), F32), shape((shots, shots, LAGS), F32)],
        in_specs=[vmem],
        out_specs=[hbm, hbm],
        scratch=[
            pltpu.VMEM((shots, rank), F32),
            pltpu.VMEM((shots, shots, LAGS), F32),
            pltpu.SemaphoreType.DMA((2,)),
        ],
        moved=2**16,
    )(terms)
    return (sketch, coarse, gram_band.transpose(0, 2, 1))


def solution(mesh):
    return jax.shard_map(
        local,
        mesh=mesh,
        in_specs=(
            P("slab", None, None),
            P("shot", "slab", None, None),
            P("shot", "slab", None, None),
            P("shot", None, "slab", None, None),
            P("shot", None, None),
            P("shot", None),
            P("shot", None),
            P("shot", None),
            P(),
            P("slab", None),
            P(),
            P(),
        ),
        out_specs=(P("shot", None), P("shot", "slab", None), P("shot", None, None)),
        check_vma=False,
    )
```

```python
import functools
import math

import jax
import jax.numpy as jnp
import ml_dtypes
import numpy as np
from jax import lax
from jax.experimental import pallas as pl
from jax.experimental.pallas import tpu as pltpu
from jax.sharding import PartitionSpec as P

LAGS = 4
REACH = 4
WHOLE_TAPS = (None, 8064.0, -1008.0, 128.0, -9.0)
DIVISOR = 5040.0
CENTRE = 3.0 * (-205.0 / 72.0)
DAMP_PEAK = 0.3
F32 = jnp.float32
BF16 = jnp.bfloat16
VMEM_BYTES = 24 * 1024 * 1024


def band_matrix(cells):
    index = np.arange(cells)
    apart = np.abs(index[:, None] - index[None, :])
    band = np.zeros((cells, cells), np.float32)
    for offset in range(1, REACH + 1):
        band[apart == offset] = WHOLE_TAPS[offset]
    return band.astype(ml_dtypes.bfloat16)


def pool_matrix(cells_y):
    half = cells_y // 2
    pool = np.zeros((2 * cells_y, 2 * half), np.float32)
    index = np.arange(cells_y)
    pool[index, index // 2] = 0.5
    pool[cells_y + index, half + index // 2] = 0.5
    return pool.astype(ml_dtypes.bfloat16)


def dot(left, right):
    return lax.dot_general(left, right, (((1,), (0,)), ((), ())), preferred_element_type=F32)


def dot_rows(left, right):
    return lax.dot_general(left, right, (((1,), (1,)), ((), ())), preferred_element_type=F32)


def two_parts(values):
    high = values.astype(BF16)
    low = (values - high.astype(F32)).astype(BF16)
    return high, low


def along_xy(planes, band_y, band_x):
    parts = [two_parts(plane) for plane in planes]
    rows = [jnp.concatenate(pair, axis=1) for pair in parts]
    columns = [jnp.concatenate(pair, axis=0) for pair in parts]
    over_y = dot(jnp.concatenate(rows, axis=0), band_y[...])
    over_x = dot(band_x[...], jnp.concatenate(columns, axis=1))
    cells_x, cells_y = planes[0].shape
    return [
        over_y[shot * cells_x : (shot + 1) * cells_x] + over_x[:, shot * cells_y : (shot + 1) * cells_y]
        for shot in range(len(planes))
    ]


def along_z(field, shot, z, cells_z):
    total = None
    for offset in range(1, REACH + 1):
        tap = WHOLE_TAPS[offset]
        below = jnp.where(z - offset >= 0, tap, 0.0)
        above = jnp.where(z + offset < cells_z, tap, 0.0)
        term = below * field[shot, jnp.maximum(z - offset, 0)]
        term += above * field[shot, jnp.minimum(z + offset, cells_z - 1)]
        total = term if total is None else total + term
    return total


def ramp_squared(index, length, thickness):
    distance = jnp.minimum(index, length - 1 - index).astype(F32)
    reach = jnp.full(index.shape, thickness, jnp.int32).astype(F32)
    ramp = jnp.maximum((reach - distance) / reach, 0.0)
    return ramp * ramp


def fetch(pairs, sems):
    copies = [
        pltpu.make_async_copy(source, target, sems.at[index])
        for index, (source, target) in enumerate(pairs)
    ]
    for copy in copies:
        copy.start()
    return copies


def begin_kernel(
    total_z,
    blocks,
    pml,
    curr_hbm,
    courant_hbm,
    prev_hbm,
    traces_hbm,
    place_z_hbm,
    place_x_hbm,
    place_y_hbm,
    band_y_hbm,
    band_x_hbm,
    updated,
    rest,
    gain_self,
    gain_lap,
    near,
    curr,
    courant,
    prev,
    traces,
    place_z,
    place_x,
    place_y,
    band_y,
    band_x,
    ramp_z,
    ramp_xy,
    inject,
    sems,
):
    cells_z, cells_x, cells_y = courant.shape
    shots = curr.shape[0]
    step = cells_z // blocks
    pairs = [
        (traces_hbm, traces),
        (place_z_hbm, place_z),
        (place_x_hbm, place_x),
        (place_y_hbm, place_y),
        (band_y_hbm, band_y),
        (band_x_hbm, band_x),
    ]
    few = len(pairs)
    for block in range(blocks):
        span = pl.ds(block * step, step)
        pairs.append((curr_hbm.at[:, span], curr.at[:, span]))
        pairs.append((courant_hbm.at[span], courant.at[span]))
        pairs.append((prev_hbm.at[:, span], prev.at[:, span]))
    copies = fetch(pairs, sems)
    first_z = lax.axis_index("slab") * cells_z
    plane = (cells_x, cells_y)
    row = lax.broadcasted_iota(jnp.int32, plane, 0)
    column = lax.broadcasted_iota(jnp.int32, plane, 1)
    ramp_z[...] = ramp_squared(
        lax.broadcasted_iota(jnp.int32, ramp_z.shape, 0) + first_z, total_z, pml[0]
    )
    ramp_xy[...] = ramp_squared(row, cells_x, pml[1]) + ramp_squared(column, cells_y, pml[2])
    for copy in copies[:few]:
        copy.wait()
    receivers = traces.shape[2]
    cell = lax.broadcasted_iota(jnp.int32, (cells_y, receivers), 0)
    for shot in range(shots):
        here = cell == place_y[shot : shot + 1, :]
        for instant in range(2):
            high, low = two_parts(jnp.where(here, traces[shot, instant : instant + 1, :], 0.0))
            span = slice(instant * cells_y, (instant + 1) * cells_y)
            inject[shot, span, :receivers] = high
            inject[shot, span, receivers:] = low
    line = lax.broadcasted_iota(jnp.int32, (cells_x, receivers), 0)

    def one_layer(z):
        damping = DAMP_PEAK * (ramp_z[pl.ds(z, 1), :] + ramp_xy[...])
        scale = 1.0 / (1.0 + damping)
        speed = courant[z]
        lap_gain = scale * (speed * speed)
        self_gain = 2.0 * scale + CENTRE * lap_gain
        lap_gain = lap_gain * (1.0 / DIVISOR)
        prev_gain = scale * (1.0 - damping)
        gain_self[z] = self_gain
        gain_lap[z] = lap_gain
        laps = along_xy([curr[shot, z] for shot in range(shots)], band_y, band_x)
        for shot in range(shots):
            now = curr[shot, z]
            lap = laps[shot] + along_z(curr, shot, z, cells_z)
            code = (place_z[shot : shot + 1, :] - first_z - z) * cells_x + place_x[shot : shot + 1, :]
            mark = jnp.where(line == code, 1.0, 0.0).astype(BF16)
            source = dot_rows(jnp.concatenate([mark, mark], axis=1), inject[shot])
            updated[shot, z] = (
                self_gain * now
                - prev_gain * prev[shot, z]
                + lap_gain * lap
                + scale * source[:, :cells_y]
            )
            rest[shot, z] = scale * source[:, cells_y:] - prev_gain * now

    layers = near.shape[1]
    near_span = pl.ds((1 - odd_slab()) * (cells_z - layers), layers)
    near_copy = pltpu.make_async_copy(
        curr_hbm.at[:, near_span], near, sems.at[few + 3 * blocks]
    )
    near_copy.start()
    copies[few].wait()
    for block in range(blocks):
        if block + 1 < blocks:
            copies[few + 3 * block + 3].wait()
        for copy in copies[few + 3 * block + 1 : few + 3 * block + 3]:
            copy.wait()
        pl.loop(block * step, (block + 1) * step)(one_layer)
    near_copy.wait()


def odd_slab():
    return lax.rem(lax.axis_index("slab"), 2)


def slice_kernel(curr, far, sems):
    layers = far.shape[1]
    last = curr.shape[1] - layers
    for copy in fetch([(curr.at[:, pl.ds(odd_slab() * last, layers)], far)], sems):
        copy.wait()


def halo_terms(halo, layer, upper):
    total = None
    for offset in range(1, REACH + 1):
        at = layer + offset - REACH if upper else layer - offset + REACH
        if 0 <= at < REACH:
            term = WHOLE_TAPS[offset] * halo(at)
            total = term if total is None else total + term
    return total


def edge_kernel(side, partial, halo, gain_lap, whole, out):
    for upper in (False, True):

        @pl.when(side[0] == int(upper))
        def _():
            @pl.loop(0, partial.shape[0])
            def _(shot):
                for layer in range(REACH):
                    terms = halo_terms(lambda at: halo[shot, at], layer, upper)
                    value = partial[shot, layer] + gain_lap[layer] * terms
                    whole[shot, layer] = value
                    out[shot, layer] = value


def emit(gradients, layer, spread_y, weight_z, pool, chunks, total, lines):
    shots = len(gradients)
    rounded = [gradient.astype(BF16) for gradient in gradients]
    cells_x = rounded[0].shape[0]
    spread = dot(jnp.concatenate(rounded, axis=0), spread_y[...])
    half = cells_x // 2
    pairs = []
    for shot in range(shots):
        total[shot] += spread[shot * cells_x : (shot + 1) * cells_x] * weight_z
        lines[shot] = rounded[shot].astype(F32)
        even = lines[shot, pl.ds(0, half, stride=2), :].astype(BF16)
        odd = lines[shot, pl.ds(1, half, stride=2), :].astype(BF16)
        pairs.append(jnp.concatenate([even, odd], axis=1))
    coarse = dot(jnp.concatenate(pairs, axis=0), pool[...])
    part = chunks.shape[2]
    pieces = half // part
    for shot in range(shots):
        for piece in range(pieces):
            start = shot * half + piece * part
            chunks[layer * pieces + piece, shot] = coarse[start : start + part]


def middle_kernel(
    blocks,
    wave,
    rest,
    gain_self,
    gain_lap,
    snaps_hbm,
    omega_z_hbm,
    omega_y_hbm,
    band_y_hbm,
    band_x_hbm,
    pool_hbm,
    panels,
    edges,
    edge_gain,
    total,
    snaps,
    omega_z,
    omega_y,
    band_y,
    band_x,
    pool,
    spread_y,
    lines,
    chunks,
    sems,
):
    shots, cells_z = wave.shape[:2]
    last = cells_z - REACH
    step = cells_z // blocks
    pairs = [
        (band_y_hbm, band_y),
        (band_x_hbm, band_x),
        (omega_y_hbm, omega_y),
        (omega_z_hbm, omega_z),
        (pool_hbm, pool),
    ]
    few = len(pairs)
    order = list(range(1, blocks - 1)) + [0, blocks - 1]
    for block in order:
        span = pl.ds(block * step, step)
        pairs.append((snaps_hbm.at[:, :, span], snaps.at[:, :, span]))
    copies = fetch(pairs, sems)
    total[...] = jnp.zeros_like(total)
    for copy in copies[:few]:
        copy.wait()
    spread_y[...] = omega_y[...].astype(F32).astype(BF16)

    def gradients_at(z):
        laps = along_xy([wave[shot, z] for shot in range(shots)], band_y, band_x)
        gradients = []
        for shot in range(shots):
            lap = laps[shot] + along_z(wave, shot, z, cells_z)
            now = wave[shot, z]
            later = gain_self[z] * now + rest[shot, z] + gain_lap[z] * lap
            gradients.append(
                now * snaps[shot, 0, z].astype(F32) + later * snaps[shot, 1, z].astype(F32)
            )
        return gradients

    def middle_layer(z):
        weight_z = omega_z[pl.ds(z, 1), :].astype(F32)
        emit(gradients_at(z), z - REACH, spread_y, weight_z, pool, chunks, total, lines)

    def edge_layer(index):
        z = index + jnp.where(index >= REACH, last - REACH, 0)
        gradients = gradients_at(z)
        for shot in range(shots):
            edges[shot, index] = gradients[shot]
            edge_gain[shot, index] = gain_lap[z] * snaps[shot, 1, z].astype(F32)

    for place, block in enumerate(order[:-2]):
        copies[few + place].wait()
        pl.loop(block * step, (block + 1) * step)(middle_layer)
    send = pltpu.make_async_copy(
        chunks, panels.at[:, :, pl.ds(0, chunks.shape[2])], sems.at[len(pairs)]
    )
    send.start()
    for copy in copies[few + blocks - 2 :]:
        copy.wait()
    pl.loop(0, 2 * REACH)(edge_layer)
    send.wait()


def finish_kernel(
    is_far,
    panels_before,
    edges,
    edge_gain,
    halo,
    omega_z,
    omega_y,
    pool,
    before,
    panels,
    total,
    spread_y,
    lines,
    chunks,
    sem,
):
    shots = edges.shape[0]
    cells_z = omega_z.shape[0]
    spread_y[...] = omega_y[...].astype(F32).astype(BF16)
    total[...] = before[...]
    part = chunks.shape[2]
    pieces = chunks.shape[0] // (2 * REACH)
    for upper in (False, True):

        @pl.when(odd_slab() == int(upper == is_far))
        def _():
            sends = []
            for layer in range(REACH):
                index = layer + (REACH if upper else 0)
                z = cells_z - REACH + layer if upper else layer
                gradients = [
                    edges[shot, index]
                    + edge_gain[shot, index]
                    * halo_terms(lambda at: halo[shot, at], layer, upper)
                    for shot in range(shots)
                ]
                weight_z = omega_z[z : z + 1, :].astype(F32)
                emit(gradients, index, spread_y, weight_z, pool, chunks, total, lines)
                span = pl.ds(index * pieces, pieces)
                send = pltpu.make_async_copy(
                    chunks.at[span], panels.at[span, :, pl.ds(part, part)], sem.at[layer]
                )
                send.start()
                sends.append(send)
            for send in sends:
                send.wait()


def sketch_kernel(total, omega_x, sketch):
    weights_x = omega_x[...].astype(F32)
    for shot in range(sketch.shape[0]):
        sketch[shot : shot + 1, :] = jnp.sum(total[shot] * weights_x, axis=0, keepdims=True)


def gram_kernel(panels, coarse, sketch, out):
    del coarse, sketch
    shots = out.shape[0]
    part = panels.shape[0] // shots
    width = 8
    gram = None
    for start in range(0, part, width):
        rows = [panels[pl.ds(start + index, shots, stride=part), :] for index in range(width)]
        high, low = two_parts(jnp.concatenate(rows, axis=1))
        both = jnp.concatenate([high, low], axis=0)
        term = dot_rows(both, both)
        gram = term if gram is None else gram + term
    folded = (gram[:shots, :shots] + gram[shots:, shots:]) + (
        gram[:shots, shots:] + gram[shots:, :shots]
    )
    out[...] = jnp.zeros_like(out)
    out[:, :shots] = folded


def gather_kernel(mine, sketch, out):
    shots = sketch.shape[0]
    total = mine[0]
    for source in range(1, mine.shape[0]):
        total = total + mine[source]
    for target in range(out.shape[0]):
        out[target, :shots] = sketch[...]
        out[target, shots:] = total


def output_kernel(
    groups, sketch_scale, gram_scale, terms, sketch_hbm, gram_hbm, sketch, gram_band, sems
):
    shots, _, lags = gram_band.shape
    lanes = terms.shape[2]
    total = terms[0]
    for source in range(1, terms.shape[0]):
        total = total + terms[source]
    sketch[...] = total[:shots] * sketch_scale
    group = lax.axis_index("shot")
    lag = lax.broadcasted_iota(jnp.int32, (lags, lanes), 0)
    lane = lax.broadcasted_iota(jnp.int32, (lags, lanes), 1)
    partner = group - 1 - lag
    partner = jnp.where(partner < 0, partner + groups, partner)
    for shot in range(shots):
        row = total[shots + shot : shots + shot + 1] * gram_scale
        for other in range(shots):
            wanted = lane == partner * shots + other
            picked = jnp.sum(jnp.where(wanted, row, 0.0), axis=1, keepdims=True)
            turned = jnp.sum(jnp.where(lane == lag, picked, 0.0), axis=0, keepdims=True)
            gram_band[shot, other : other + 1, :] = turned[:, :lags]
    for copy in fetch([(sketch, sketch_hbm), (gram_band, gram_hbm)], sems):
        copy.wait()


def spec(block=None, index=None):
    if block is None:
        return pl.BlockSpec(memory_space=pltpu.VMEM)
    return pl.BlockSpec(block, lambda step: index)


def run(kernel, out_shape, in_specs, out_specs, scratch=(), flops=0, moved=0, grid=None, **options):
    if grid is not None:
        options["grid"] = grid
    return pl.pallas_call(
        kernel,
        out_shape=out_shape,
        in_specs=in_specs,
        out_specs=out_specs,
        scratch_shapes=scratch,
        compiler_params=pltpu.CompilerParams(vmem_limit_bytes=VMEM_BYTES),
        cost_estimate=pl.CostEstimate(flops=flops, bytes_accessed=moved, transcendentals=0),
        **options,
    )


def local(
    courant,
    adj_prev,
    adj_curr,
    forward_snaps,
    traces,
    receiver_z,
    receiver_x,
    receiver_y,
    pml_cells,
    omega_z,
    omega_x,
    omega_y,
):
    shots, cells_z, cells_x, cells_y = adj_curr.shape
    slabs = lax.axis_size("slab")
    groups = lax.axis_size("shot")
    total_z = cells_z * slabs
    last = cells_z - REACH
    inner = last - REACH
    rank = omega_z.shape[1]
    receivers = traces.shape[2]
    half_x = cells_x // 2
    part = inner * half_x // groups
    blocks = cells_z // REACH
    shape = jax.ShapeDtypeStruct
    plane = (cells_x, cells_y)
    band = band_matrix(cells_y)
    band_y = jnp.asarray(np.concatenate([band, band], axis=0))
    band = band_matrix(cells_x)
    band_x = jnp.asarray(np.concatenate([band, band], axis=1))
    pool = jnp.asarray(pool_matrix(cells_y))

    def with_near(layers):
        return lax.ppermute(layers, "slab", [(i, i ^ 1) for i in range(slabs)])

    def with_far(layers):
        pairs = [(i, i + 1) for i in range(1, slabs - 1, 2)]
        return lax.ppermute(layers, "slab", pairs + [(j, i) for i, j in pairs])

    vmem = spec()
    hbm = pl.BlockSpec(memory_space=pltpu.HBM)

    def pinned(*arrays):
        return [pltpu.with_memory_space_constraint(array, pltpu.HBM) for array in arrays]

    field = shape((shots, cells_z) + plane, F32)
    gain = shape((cells_z,) + plane, F32)
    edge = shape((shots, REACH) + plane, F32)
    like = lambda array: pltpu.VMEM(array.shape, array.dtype)
    far = run(
        slice_kernel,
        edge,
        in_specs=[hbm],
        out_specs=vmem,
        scratch=[pltpu.SemaphoreType.DMA((1,))],
        moved=2**20,
    )(*pinned(adj_curr))
    far = with_far(far)
    updated, rest, gain_self, gain_lap, near = run(
        functools.partial(begin_kernel, total_z, blocks),
        [field, field, gain, gain, edge],
        in_specs=[pl.BlockSpec(memory_space=pltpu.SMEM)] + [hbm] * 9,
        out_specs=[vmem] * 5,
        scratch=[
            like(adj_curr),
            like(courant),
            like(adj_prev),
            like(traces),
            like(receiver_z),
            like(receiver_x),
            like(receiver_y),
            like(band_y),
            like(band_x),
            pltpu.VMEM((cells_z, cells_y), F32),
            pltpu.VMEM(plane, F32),
            pltpu.VMEM((shots, 2 * cells_y, 2 * receivers), BF16),
            pltpu.SemaphoreType.DMA((7 + 3 * blocks,)),
        ],
        flops=2 * 10**9,
        moved=11 * 2**20,
    )(
        pml_cells,
        *pinned(
            adj_curr,
            courant,
            adj_prev,
            traces,
            receiver_z,
            receiver_x,
            receiver_y,
            band_y,
            band_x,
        ),
    )

    layers4 = (shots, REACH) + plane
    gains4 = (REACH,) + plane

    whole4 = pl.BlockSpec(layers4, lambda step, side: (0, 0, 0, 0))
    wave4 = pl.BlockSpec(layers4, lambda step, side: (0, side[0] * (blocks - 1), 0, 0))

    def complete(side, wave, halo):
        return pl.pallas_call(
            edge_kernel,
            out_shape=[field, edge],
            grid_spec=pltpu.PrefetchScalarGridSpec(
                num_scalar_prefetch=1,
                grid=(1,),
                in_specs=[
                    wave4,
                    whole4,
                    pl.BlockSpec(gains4, lambda step, side: (side[0] * (blocks - 1), 0, 0)),
                ],
                out_specs=[wave4, whole4],
            ),
            compiler_params=pltpu.CompilerParams(vmem_limit_bytes=VMEM_BYTES),
            cost_estimate=pl.CostEstimate(
                flops=10**7, bytes_accessed=2 * 2**20, transcendentals=0
            ),
            input_output_aliases={1: 0},
        )(side, wave, halo, gain_lap)

    side = jnp.remainder(lax.axis_index("slab"), 2).astype(jnp.int32).reshape(1)
    near = with_near(near)
    wave, near = complete(1 - side, updated, near)
    wave, far = complete(side, wave, far)
    far = with_far(far)
    near = with_near(near)

    panel = shape((groups, shots, 2 * part, cells_y), F32)
    spread = shape((shots, cells_x, rank), F32)
    scratch_emit = [
        pltpu.VMEM((cells_y, rank), BF16),
        pltpu.VMEM((shots,) + plane, F32),
        pltpu.VMEM((groups, shots, part, cells_y), F32),
    ]
    both = shape((shots, 2 * REACH) + plane, F32)
    panels, edges, edge_gain, total_mid = run(
        functools.partial(middle_kernel, blocks),
        [panel, both, both, spread],
        in_specs=[vmem] * 4 + [hbm] * 6,
        out_specs=[hbm, vmem, vmem, vmem],
        scratch=[
            like(forward_snaps),
            like(omega_z),
            like(omega_y),
            like(band_y),
            like(band_x),
            like(pool),
        ]
        + scratch_emit
        + [pltpu.SemaphoreType.DMA((6 + blocks,))],
        flops=2 * 10**9,
        moved=11 * 2**20,
    )(
        wave,
        rest,
        gain_self,
        gain_lap,
        *pinned(forward_snaps, omega_z, omega_y, band_y, band_x, pool),
    )

    def finish(is_far, panels, halo, total):
        return run(
            functools.partial(finish_kernel, is_far),
            [panel, spread],
            in_specs=[hbm] + [vmem] * 7,
            out_specs=[hbm, vmem],
            scratch=scratch_emit + [pltpu.SemaphoreType.DMA((REACH,))],
            flops=3 * 10**8,
            moved=3 * 2**20,
            input_output_aliases={0: 0},
        )(panels, edges, edge_gain, halo, omega_z, omega_y, pool, total)

    panels, total = finish(False, panels, near, total_mid)
    panels, total = finish(True, panels, far, total)
    sketch_part = run(
        sketch_kernel,
        shape((shots, rank), F32),
        in_specs=[vmem, vmem],
        out_specs=vmem,
        flops=2 * 10**5,
        moved=2**18,
    )(total, omega_x)
    got = lax.all_to_all(panels, "shot", 0, 0, tiled=True)

    folded = panels.reshape(inner, half_x // part, shots, 2, part, cells_y)
    folded = folded.transpose(3, 2, 0, 1, 4, 5).reshape(2, shots, inner, half_x, cells_y)
    coarse = jnp.concatenate(
        [folded[1, :, :REACH], folded[0], folded[1, :, REACH:]], axis=1
    ).reshape(shots, cells_z, half_x * cells_y)

    all_shots = groups * shots
    gram = run(
        gram_kernel,
        shape((all_shots, cells_y), F32),
        in_specs=[vmem, hbm, hbm],
        out_specs=vmem,
        flops=10**8,
        moved=2**20,
    )(got.reshape(all_shots * 2 * part, cells_y), *pinned(coarse, sketch_part))
    mine = lax.all_to_all(gram.reshape(groups, shots, cells_y), "shot", 0, 0, tiled=True)
    terms = run(
        gather_kernel,
        shape((slabs, 2 * shots, rank), F32),
        in_specs=[vmem, vmem],
        out_specs=vmem,
        moved=2**16,
    )(mine, sketch_part)
    terms = lax.all_to_all(terms, "slab", 0, 0, tiled=True)
    sketch, gram_band = run(
        functools.partial(
            output_kernel,
            groups,
            1.0 / math.sqrt(total_z * cells_x * cells_y),
            1.0 / math.sqrt(total_z * cells_x * cells_y // 2),
        ),
        [shape((shots, rank), F32), shape((shots, shots, LAGS), F32)],
        in_specs=[vmem],
        out_specs=[hbm, hbm],
        scratch=[
            pltpu.VMEM((shots, rank), F32),
            pltpu.VMEM((shots, shots, LAGS), F32),
            pltpu.SemaphoreType.DMA((2,)),
        ],
        moved=2**16,
    )(terms)
    return (sketch, coarse, gram_band.transpose(0, 2, 1))


def solution(mesh):
    return jax.shard_map(
        local,
        mesh=mesh,
        in_specs=(
            P("slab", None, None),
            P("shot", "slab", None, None),
            P("shot", "slab", None, None),
            P("shot", None, "slab", None, None),
            P("shot", None, None),
            P("shot", None),
            P("shot", None),
            P("shot", None),
            P(),
            P("slab", None),
            P(),
            P(),
        ),
        out_specs=(P("shot", None), P("shot", "slab", None), P("shot", None, None)),
        check_vma=False,
    )
```
